32 devices in a mesh: grp: 2 (over y), blk: 8 (over z, x), pair: 2 (over core).
Axes of the slice: x: 2, y: 2, z: 4, core: 2. Of those that a mesh axis runs over, the one named last changes fastest.
Arguments:
- wavefunc: bfloat16 [96, 16, 2, 768], P(('grp', 'blk')), parts along dimension 0, may hold values from -6 to 6
- haydock: float32 [96, 128], P(('grp', 'blk')), parts along dimension 0, may hold values from -6 to 6
- screened: bfloat16 [16, 768, 768], P(('grp', 'blk')), parts along dimension 0, may hold values from -0.21875 to 0.21875
- coulomb: float32 [1536], P('grp'), parts along dimension 0, may hold values from 0.05 to 1
- umklapp_map: int32 [3, 768], replicated, may hold values from 0 to 767, each once within a row
Outputs:
- kernel_out: float32 [96, 128], P(('grp', 'blk')), parts along dimension 0
The draws below stay inside these ranges and needn't reach their ends.
There are 2 independent parts, one for each index of `grp`. The reference program is written for one: setup_inputs(seed, part) draws one part's arguments, and reference() takes and returns one part's arrays. A program takes and returns all parts, laid end to end along the dimension named above; an argument that names none is the same for every part. Nothing has to cross between parts.
Inputs may be any that keep to these rules, and one draw needn't show every extreme that they name: Each row of umklapp_map is a permutation of 0 .. 767.
All inputs are finite; a program needn't handle non-finite values.
Results may differ from the reference program's by a relative error of at most 0.015.
Values may be sent and summed in bfloat16 or wider, within the bound.
A program may use at most 64 MiB of HBM per device.

```python
import math
import jax
import jax.numpy as jnp
from jax import lax

NV = 8
NC = 8
NG = 768
KR = 6
STOPS = 2
NB = 16
QS = 8
NK = 48
NPSI = 128


def levels(key, extent, cuts, low, largest):
    factor_of, own = 1.0, jax.random.fold_in(key, 6)
    for dim, parts in cuts:
        heights = jnp.exp(jax.random.uniform(jax.random.fold_in(own, dim), (parts,), jnp.float32, low / len(cuts), largest / len(cuts)))
        factor_of = factor_of * jnp.repeat(heights, extent[dim] // parts).reshape([-1 if axis == dim else 1 for axis in range(len(extent))])
    return factor_of


def noise(own_key, dims, spread, limit, pieces=(), kind=jnp.bfloat16):
    factor_of = levels(own_key, dims, pieces, -0.22, 0.18) if pieces else 1.0
    drawn = jax.random.normal(own_key, dims, jnp.float32) * spread * factor_of
    return jnp.minimum(jnp.maximum(drawn, -limit), limit).astype(kind)


def setup_inputs(seed: int = 0, part: int = 0) -> dict:
    keys = jax.random.split(jax.random.key(seed), 6)
    own_keys = jax.random.split(jax.random.fold_in(keys[5], part), 6)
    return {
        "wavefunc": noise(own_keys[0], (NK, NB, 2, NG), 1.0, 6.0, ((0, 8),)),
        "haydock": noise(own_keys[1], (NK, NPSI), 1.0, 6.0, ((0, 8),), jnp.float32),
        "screened": noise(own_keys[2], (QS, NG, NG), NG ** -0.5, 0.21875, ((0, 8),)),
        "coulomb": jnp.clip(jnp.exp(jax.random.uniform(own_keys[3], (NG,), jnp.float32, math.log(0.05), math.log(1.0))), 0.05, 1.0),
        "umklapp_map": jax.vmap(lambda own: jax.random.permutation(own, NG))(jax.random.split(keys[4], (STOPS + 1))).reshape((STOPS + 1, NG)).astype(jnp.int32),
    }


def make_amplitude(wave_rows, amp_rows):
    count = wave_rows.shape[0]
    valence = wave_rows[:, :NV].astype(jnp.float32)
    val_re = valence[:, :, 0]
    val_im = valence[:, :, 1]
    amps = amp_rows.reshape(count, 2, NV, NC)
    amp_re = amps[:, 0]
    amp_im = amps[:, 1]
    out_re = jnp.einsum('kvg,kvc->kcg', val_re, amp_re) - jnp.einsum('kvg,kvc->kcg', val_im, amp_im)
    out_im = jnp.einsum('kvg,kvc->kcg', val_re, amp_im) + jnp.einsum('kvg,kvc->kcg', val_im, amp_re)
    return jnp.stack([out_re, out_im], axis=2).astype(jnp.bfloat16)

def densities(wave_rows):
    wide = wave_rows.astype(jnp.float32)
    val_re = wide[:, :NV, 0][:, :, None, :]
    val_im = wide[:, :NV, 1][:, :, None, :]
    cond_re = wide[:, NV:, 0][:, None, :, :]
    cond_im = wide[:, NV:, 1][:, None, :, :]
    return (val_re * cond_re + val_im * cond_im, val_re * cond_im - val_im * cond_re)

def fold_exchange(dens_re, dens_im, amp_rows):
    count = amp_rows.shape[0]
    amps = amp_rows.reshape(count, 2, NV, NC)
    amp_re = amps[:, 0]
    amp_im = amps[:, 1]
    x_re = jnp.einsum('kvcg,kvc->g', dens_re, amp_re) + jnp.einsum('kvcg,kvc->g', dens_im, amp_im)
    x_im = jnp.einsum('kvcg,kvc->g', dens_re, amp_im) - jnp.einsum('kvcg,kvc->g', dens_im, amp_re)
    return (x_re, x_im)

def exchange_terms(dens_re, dens_im, x_re, x_im, coulomb):
    count = dens_re.shape[0]
    y_re = coulomb * x_re
    y_im = coulomb * x_im
    out_re = jnp.einsum('kvcg,g->kvc', dens_re, y_re) - jnp.einsum('kvcg,g->kvc', dens_im, y_im)
    out_im = jnp.einsum('kvcg,g->kvc', dens_re, y_im) + jnp.einsum('kvcg,g->kvc', dens_im, y_re)
    return jnp.stack([out_re, out_im], axis=1).reshape(count, -1)

def direct_fold(wave_rows, permuted, weight):
    valence = wave_rows[:, :NV].astype(jnp.float32)
    val_re = valence[:, :, 0][:, None, :, None, :]
    val_im = valence[:, :, 1][:, None, :, None, :]
    wide = permuted.astype(jnp.float32)
    ahat_re = wide[:, :NC, 0][None, :, None, :, :]
    ahat_im = wide[:, :NC, 1][None, :, None, :, :]
    cond_re = wide[:, NC:, 0]
    cond_im = wide[:, NC:, 1]
    y_re = val_re * ahat_re + val_im * ahat_im
    y_im = val_re * ahat_im - val_im * ahat_re
    stacked = jnp.stack([y_re, y_im], axis=4).astype(jnp.bfloat16)
    flat = stacked.reshape(-1, weight.shape[1])
    image = jnp.dot(flat, weight.T, preferred_element_type=jnp.float32).reshape(stacked.shape)
    z_re = image[:, :, :, :, 0]
    z_im = image[:, :, :, :, 1]
    e_re = jnp.einsum('kjvcg,jcg->kvg', z_re, cond_re) + jnp.einsum('kjvcg,jcg->kvg', z_im, cond_im)
    e_im = jnp.einsum('kjvcg,jcg->kvg', z_im, cond_re) - jnp.einsum('kjvcg,jcg->kvg', z_re, cond_im)
    return (e_re, e_im)

def finish(wave_rows, e_re, e_im):
    count = wave_rows.shape[0]
    cond = wave_rows[:, NV:].astype(jnp.float32)
    cond_re = cond[:, :, 0]
    cond_im = cond[:, :, 1]
    out_re = jnp.einsum('kcg,kvg->kvc', cond_re, e_re) - jnp.einsum('kcg,kvg->kvc', cond_im, e_im)
    out_im = jnp.einsum('kcg,kvg->kvc', cond_re, e_im) + jnp.einsum('kcg,kvg->kvc', cond_im, e_re)
    return jnp.stack([out_re, out_im], axis=1).reshape(count, -1)

def reference(wavefunc, haydock, screened, coulomb, umklapp_map):
    total = wavefunc.shape[0]
    amplitude = make_amplitude(wavefunc, haydock)
    partner = jnp.concatenate([amplitude, wavefunc[:, NV:]], axis=1)
    dens_re, dens_im = densities(wavefunc)
    x_re, x_im = fold_exchange(dens_re, dens_im, haydock)
    exchange = exchange_terms(dens_re, dens_im, x_re, x_im, coulomb) * (1.0 / (8.0 * math.sqrt(NG * NK)))
    scale_direct = -1.0 / (8.0 * math.sqrt(NG * KR * (STOPS + 1)))

    def per_block(block):
        rows_now = lax.dynamic_slice_in_dim(wavefunc, (block * KR).astype(jnp.int32), KR, 0)
        e_re = jnp.zeros((KR, NV, NG), jnp.float32)
        e_im = jnp.zeros((KR, NV, NG), jnp.float32)
        for stop_index in range(STOPS + 1):
            source = ((block - stop_index) % QS * KR).astype(jnp.int32)
            part_rows = lax.dynamic_slice_in_dim(partner, source, KR, 0)
            permuted = jnp.take(part_rows, umklapp_map[stop_index], axis=3)
            d_re, d_im = direct_fold(rows_now, permuted, screened[stop_index])
            e_re = e_re + d_re
            e_im = e_im + d_im
        return finish(rows_now, e_re, e_im)
    direct = lax.map(per_block, jnp.arange(QS, dtype=jnp.int32))
    direct = direct.reshape(total, -1) * scale_direct
    return direct + exchange
```

```python
import functools
import math

import jax
import jax.numpy as jnp
from jax import lax
from jax.experimental import pallas as pl
from jax.experimental.pallas import tpu as pltpu
from jax.sharding import PartitionSpec as P

NV = 8
NC = 8
STOPS = 2
MESH = pl.DeviceIdType.MESH
NT = (((1,), (1,)), ((), ()))

OWN = {
    0: ((1, 0), (1, 1), (2, 0)),
    1: ((0, 1), (2, 1)),
    2: ((0, 0),),
    3: ((1, 0), (2, 1)),
    4: ((0, 0), (2, 0)),
    5: ((1, 1), (2, 1)),
    6: ((2, 0), (0, 0)),
    7: ((1, 1), (2, 1)),
}
UNITS = {
    (0, 0): ((0, ()), (2, ((2, (1, 0)),)), (4, ((4, (1, 1)),)), (6, ((6, (1, 1)),))),
    (0, 1): ((1, ((1, None),)), (3, ((3, None),)), (5, ((5, None),)), (7, ((7, None),))),
    (1, 0): ((0, ((0, None),)), (1, ((3, (0, 1)), (2, None))), (2, ()), (3, ((4, None),))),
    (1, 1): ((7, ((0, None), (5, (0, 1)), (7, (0, 1)))), (4, ((4, (1, 0)),)), (5, ((6, None),)), (6, ())),
    (2, 0): ((0, ((0, None),)), (2, ((4, None),)), (6, ((6, None),)), (4, ())),
    (2, 1): ((1, ((1, None), (3, None))), (3, ((5, None),)), (7, ((7, None),)), (5, ())),
}
HUB = (0, 1)
ACTIONS = 3


def edges():
    to = {}
    for blk, targets in OWN.items():
        for target in targets:
            for core in range(2):
                to.setdefault(target, set()).add((blk, core))
    for worker, units in UNITS.items():
        for _, actions in units:
            for _, target in actions:
                if target is not None:
                    to.setdefault(target, set()).add(worker)
    for blk in range(8):
        for core in range(2):
            if (blk, core) != HUB:
                to.setdefault(HUB, set()).add((blk, core))
    for blk in range(STOPS + 1):
        to.setdefault((blk, 1), set()).add((blk, 0))
    return to


def dot_nt(a, b):
    return lax.dot_general(a, b, NT, preferred_element_type=jnp.float32)


def dot_nn(a, b):
    return jnp.dot(a, b, preferred_element_type=jnp.float32)


def lut(index, values):
    out = jnp.int32(0)
    for n, value in enumerate(values):
        if value:
            out = jnp.where(index == n, jnp.int32(value), out)
    return out


def iota(shape, dim):
    return lax.broadcasted_iota(jnp.int32, shape, dim)


def spread_matrix(edge):
    half = edge
    row, col = iota((128, 256), 0), iota((128, 256), 1)
    lane = col % 128
    y = (lane >= half).astype(jnp.int32)
    part = jnp.where(col >= 128, 1 - y, y)
    return ((row // 64 == part) & ((row % 64) // NC == lane % NV)).astype(jnp.bfloat16)


def make_mix(hay, spread, count):
    edge = count * NV
    tall = jnp.concatenate(
        [jnp.broadcast_to(hay[k : k + 1, :], (NC, 128)) for _ in range(2) for k in range(count)], axis=0
    )
    shape = (2 * edge, 128)
    row, col = iota(shape, 0), iota(shape, 1)
    tall = jnp.where(row % NC == col % NC, tall, 0.0).astype(jnp.bfloat16)
    q = dot_nn(tall, spread)
    top = row < edge
    k_row = jnp.where(top, row, row - edge) // NC
    k_col = jnp.where(col < edge, col, col - edge) // NV
    mix = jnp.where(top, jnp.where(col < edge, q[:, :128], -q[:, :128]), q[:, 128:])
    keep = (k_row == k_col) & (col < 2 * edge)
    return jnp.where(keep, mix, 0.0).astype(jnp.bfloat16)[:, : 2 * edge]


def fold_block(t, count):
    edge = count * NV
    row, col = iota(t.shape, 0), iota(t.shape, 1)
    k_row = jnp.where(row < edge, row, row - edge) // NC
    k_col = jnp.where(col < edge, col, col - edge) // NV
    t = jnp.where(k_row == k_col, t, 0.0)
    halves = []
    for x in range(2):
        acc = t[x * edge : x * edge + NC]
        for k in range(1, count):
            acc = acc + t[x * edge + k * NC : x * edge + (k + 1) * NC]
        halves.append(acc)
    return jnp.concatenate(halves, axis=0)


def lay_out(total, count):
    edge = count * NV
    z0 = jnp.concatenate([total[:NC]] * 16, axis=0)
    z1 = jnp.concatenate([total[NC:]] * 16, axis=0)
    shape = z0.shape
    row, col = iota(shape, 0), iota(shape, 1)
    y0 = col < edge
    z = jnp.where(row < 64, jnp.where(y0, z0, -z1), jnp.where(y0, z1, z0))
    z = jnp.where((row % 64) // NC == col % NV, z, 0.0)
    high = z.astype(jnp.bfloat16)
    low = (z - high.astype(jnp.float32)).astype(jnp.bfloat16)
    krow, kcol = iota((8, shape[1]), 0), iota((8, shape[1]), 1)
    pick = (jnp.where(kcol < edge, kcol, kcol - edge) // NV == krow).astype(jnp.bfloat16)
    return dot_nt(pick, high) + dot_nt(pick, low)


def kernel(
    count, scale_d, scale_x,
    piece_ref, hay_ref, weight_ref, map_ref, coul_ref, out_ref,
    vbuf, cbuf, hbuf, wbuf, sel, fbuf, spread, stage, res, xbuf, ybuf,
    load_sem, recv_sem, send_own, send_rel, send_res, recv_res, send_x, recv_x, send_y, recv_y,
):
    grp = lax.axis_index("grp")
    me = lax.axis_index("blk")
    p = lax.axis_index("pair")
    blocks = lax.axis_size("blk")
    dev = me * 2 + p
    planes = weight_ref.shape[1]
    edge = count * NV
    hub = HUB[0] * 2 + HUB[1]
    worker = me < STOPS + 1

    barrier = pltpu.get_barrier_semaphore()
    to = edges()
    expect = [0] * 16
    for (blk, core), senders in to.items():
        for sender in senders:
            expect[sender[0] * 2 + sender[1]] += 1

        @pl.when(dev == blk * 2 + core)
        def _():
            for sender in sorted(senders):
                pl.semaphore_signal(
                    barrier, inc=1, device_id=(grp, sender[0], sender[1]), device_id_type=MESH
                )

    load = pltpu.make_async_copy(weight_ref.at[0], wbuf, load_sem)

    @pl.when(worker)
    def _():
        load.start()

    hbuf[me, :count] = hay_ref[...]
    hbuf[me, count:] = jnp.zeros((8 - count, 128), jnp.float32)
    pl.semaphore_wait(barrier, lut(dev, expect))

    def own_copy(kind, slot):
        targets = [(OWN[m] + (None,) * 3)[slot] for m in range(8)]
        code = lut(me, [0 if t is None else t[0] * 2 + t[1] + 1 for t in targets])
        target = jnp.maximum(code - 1, 0)
        src, dst = ((piece_ref.at[0], vbuf), (piece_ref.at[1], cbuf), (hbuf.at[me], hbuf))[kind]
        return code > 0, pltpu.make_async_remote_copy(
            src_ref=src,
            dst_ref=dst.at[me],
            send_sem=send_own.at[kind, slot],
            recv_sem=recv_sem.at[kind, me],
            device_id=(grp, target // 2, target % 2),
            device_id_type=MESH,
        )

    def own_copies(act):
        for slot in range(3):
            for kind, core in ((2, 0), (0, 0), (1, 1)):
                go, copy = own_copy(kind, slot)

                @pl.when(go & (p == core))
                def _():
                    act(copy)

    own_copies(lambda copy: copy.start())

    vbuf[me] = piece_ref[0]
    cbuf[me] = piece_ref[1]
    spread[...] = spread_matrix(edge)
    mix = make_mix(hbuf[me], spread[...], count)
    amp = dot_nn(mix, piece_ref[0])
    cond_own = piece_ref[1].astype(jnp.float32)
    c_re, c_im = cond_own[:edge], cond_own[edge:]
    a_re, a_im = amp[:edge], amp[edge:]
    xbuf[dev, 0:1, :] = jnp.sum(c_re * a_re + c_im * a_im, axis=0, keepdims=True)
    xbuf[dev, 1:2, :] = jnp.sum(c_re * a_im - c_im * a_re, axis=0, keepdims=True)

    x_copy = pltpu.make_async_remote_copy(
        src_ref=xbuf.at[dev],
        dst_ref=xbuf.at[dev],
        send_sem=send_x,
        recv_sem=recv_x.at[dev],
        device_id=(grp, HUB[0], HUB[1]),
        device_id_type=MESH,
    )

    def y_copy(other):
        return pltpu.make_async_remote_copy(
            src_ref=ybuf,
            dst_ref=ybuf,
            send_sem=send_y.at[other],
            recv_sem=recv_y,
            device_id=(grp, other // 2, other % 2),
            device_id_type=MESH,
        )

    @pl.when(dev != hub)
    def _():
        x_copy.start()

    def whole(kind, b):
        return (vbuf.at[b], cbuf.at[b], hbuf.at[b])[kind]

    def relay(kind, b, target):
        return pltpu.make_async_remote_copy(
            src_ref=whole(kind, b),
            dst_ref=whole(kind, b),
            send_sem=send_rel.at[kind, b],
            recv_sem=recv_sem.at[kind, b],
            device_id=(grp, target // 2, target % 2),
            device_id_type=MESH,
        )

    def res_copy(t, b, s, core):
        return pltpu.make_async_remote_copy(
            src_ref=stage.at[t],
            dst_ref=res.at[s],
            send_sem=send_res.at[t, core],
            recv_sem=recv_res.at[s],
            device_id=(grp, b, core),
            device_id_type=MESH,
        )

    def unit_of(t):
        at = dev * 4 + t
        partner = [0] * 24
        for (s, core), units in UNITS.items():
            for step, (i, _) in enumerate(units):
                partner[(s * 2 + core) * 4 + step] = i
        i = lut(at, partner)
        return i, (i + me) % blocks

    def action_of(t, n):
        codes = [0] * 24
        for (s, core), units in UNITS.items():
            for step, (_, actions) in enumerate(units):
                if n < len(actions):
                    b, target = actions[n]
                    onward = 0 if target is None else target[0] * 2 + target[1] + 1
                    codes[(s * 2 + core) * 4 + step] = 1 + b + 8 * onward
        code = lut(dev * 4 + t, codes)
        packed = jnp.maximum(code - 1, 0)
        return code > 0, packed % 8, packed // 8

    @pl.when(worker)
    def _():
        sel[...] = jnp.where(
            map_ref[pl.ds(me, 1), :] == iota((planes, planes), 0), 1.0, 0.0
        ).astype(jnp.bfloat16)
        load.wait()

        def step(t, carry):
            @pl.when((dev == hub) & (t == 1))
            def _():
                for d in range(16):
                    if d != hub:
                        pltpu.make_async_copy(xbuf.at[d], xbuf.at[d], recv_x.at[d]).wait()
                ybuf[...] = jnp.sum(xbuf[...], axis=0) * coul_ref[...] * (0.5 * scale_x)
                for d in range(16):
                    if d != hub:
                        y_copy(d).start()

            for n in range(ACTIONS):
                go, b, onward = action_of(t, n)

                @pl.when(go)
                def _():
                    for kind in (2, 0, 1):
                        pltpu.make_async_copy(whole(kind, b), whole(kind, b), recv_sem.at[kind, b]).wait()

                        @pl.when(onward > 0)
                        def _():
                            relay(kind, b, jnp.maximum(onward - 1, 0)).start()

            i, b = unit_of(t)
            mix_i = make_mix(hbuf[i], spread[...], count)
            amp_i = dot_nn(mix_i, vbuf[i]).astype(jnp.bfloat16)
            perm = dot_nn(jnp.concatenate([amp_i, cbuf[i]], axis=0), sel[...])
            cond_t = perm[2 * edge :].T.astype(jnp.bfloat16)
            turned = jnp.concatenate([perm[edge : 2 * edge], -perm[:edge]], axis=0)
            both = jnp.concatenate([perm[: 2 * edge], turned], axis=1).astype(jnp.bfloat16)
            val_b = vbuf[b]
            swapped = jnp.concatenate([-val_b[edge:], val_b[:edge]], axis=0)
            v_lanes = jnp.concatenate(
                [
                    jnp.concatenate([val_b[:edge], swapped[:edge]], axis=0),
                    jnp.concatenate([val_b[edge:], swapped[edge:]], axis=0),
                ],
                axis=1,
            )
            tile = 256
            for r in range(planes // tile):
                rows = slice(r * tile, (r + 1) * tile)
                w = wbuf[rows, :].astype(jnp.float32)
                h = (dot_nn(cond_t[rows], both) * jnp.concatenate([w, w], axis=1)).astype(jnp.bfloat16)
                fbuf[rows, :] = dot_nt(h, v_lanes).astype(jnp.bfloat16)
            part = fold_block(dot_nn(cbuf[b], fbuf[...]), count) * scale_d
            stage[t, :, : 2 * edge] = part
            for core in range(2):
                mine = (b == me) & (p == core)

                @pl.when(mine)
                def _():
                    res[me, :, : 2 * edge] = part

                @pl.when(jnp.logical_not(mine))
                def _():
                    res_copy(t, b, me, core).start()

            return carry

        lax.fori_loop(0, 4, step, 0)

    @pl.when(dev != hub)
    def _():
        pltpu.make_async_copy(ybuf, ybuf, recv_y).wait()

    y_re, y_im = ybuf[0:1, :], ybuf[1:2, :]
    v_re = piece_ref[0, :edge].astype(jnp.float32)
    v_im = piece_ref[0, edge:].astype(jnp.float32)
    f_rows = jnp.concatenate([y_re * v_re + y_im * v_im, y_im * v_re - y_re * v_im], axis=0)
    total = fold_block(dot_nt(piece_ref[1], f_rows.astype(jnp.bfloat16)), count)

    for s in range(STOPS + 1):
        @pl.when(jnp.logical_not((me == s) & (p == 0)))
        def _():
            pltpu.make_async_copy(res.at[s], res.at[s], recv_res.at[s]).wait()
    for s in range(STOPS + 1):
        total = total + res[s, :, : 2 * edge]
    out_ref[...] = lay_out(total, count)[:count]

    own_copies(lambda copy: copy.wait_send())

    @pl.when(dev != hub)
    def _():
        x_copy.wait_send()

    @pl.when(dev == hub)
    def _():
        for d in range(16):
            if d != hub:
                y_copy(d).wait_send()

    @pl.when(worker)
    def _():
        def drain(t, carry):
            for n in range(ACTIONS):
                go, b, onward = action_of(t, n)

                @pl.when(go & (onward > 0))
                def _():
                    for kind in range(3):
                        relay(kind, b, jnp.maximum(onward - 1, 0)).wait_send()
            _, b = unit_of(t)
            for core in range(2):
                @pl.when(jnp.logical_not((b == me) & (p == core)))
                def _():
                    res_copy(t, b, me, core).wait_send()
            return carry

        lax.fori_loop(0, 4, drain, 0)


def scales(planes, count, total_k):
    return (
        -1.0 / (8.0 * math.sqrt(planes * count * (STOPS + 1))),
        1.0 / (8.0 * math.sqrt(planes * total_k)),
    )


def rows_of(wave):
    count, _, _, planes = wave.shape
    rows = wave.reshape(count, 2, NV, 2, planes).transpose(1, 3, 0, 2, 4)
    return rows.reshape(2, 2 * count * NV, planes)


def per_device(wavefunc, haydock, screened, coulomb, umklapp_map):
    count, _, _, planes = wavefunc.shape
    blocks = lax.axis_size("blk")
    edge = count * NV
    scale_d, scale_x = scales(planes, count, count * blocks)
    vmem = pl.BlockSpec(memory_space=pltpu.VMEM)
    dma = pltpu.SemaphoreType.DMA
    return pl.pallas_call(
        functools.partial(kernel, count, scale_d, scale_x),
        out_shape=jax.ShapeDtypeStruct((count, 128), jnp.float32),
        in_specs=[vmem, vmem, pl.BlockSpec(memory_space=pl.ANY), vmem, vmem],
        out_specs=vmem,
        scratch_shapes=[
            pltpu.VMEM((blocks, 2 * edge, planes), jnp.bfloat16),
            pltpu.VMEM((blocks, 2 * edge, planes), jnp.bfloat16),
            pltpu.VMEM((blocks, 8, 128), jnp.float32),
            pltpu.VMEM((planes, planes), jnp.bfloat16),
            pltpu.VMEM((planes, planes), jnp.bfloat16),
            pltpu.VMEM((planes, 2 * edge), jnp.bfloat16),
            pltpu.VMEM((128, 256), jnp.bfloat16),
            pltpu.VMEM((4, 2 * NV, 128), jnp.float32),
            pltpu.VMEM((STOPS + 1, 2 * NV, 128), jnp.float32),
            pltpu.VMEM((2 * blocks, 2, planes), jnp.float32),
            pltpu.VMEM((2, planes), jnp.float32),
            dma,
            dma((3, blocks)),
            dma((3, 3)),
            dma((3, blocks)),
            dma((4, 2)),
            dma((STOPS + 1,)),
            dma,
            dma((2 * blocks,)),
            dma((2 * blocks,)),
            dma,
        ],
        compiler_params=pltpu.CompilerParams(
            collective_id=0, has_side_effects=True, vmem_limit_bytes=40 * 1024 * 1024
        ),
    )(rows_of(wavefunc), haydock, screened, umklapp_map, coulomb.reshape(1, planes))


def make_pieces(wave, hay):
    count, bands, _, planes = wave.shape
    rows = wave.reshape(count, 2, NV, 2, planes).transpose(1, 3, 0, 2, 4)
    rows = rows.reshape(2, 2 * count * NV, planes)
    psi = hay.reshape(count, 2, NV, NC).transpose(1, 0, 3, 2)
    eye = jnp.eye(count, dtype=jnp.float32)
    wide = (psi[:, :, :, None, :] * eye[None, :, None, :, None]).reshape(2, count * NC, count * NV)
    top = jnp.concatenate([wide[0], -wide[1]], axis=1)
    low = jnp.concatenate([wide[1], wide[0]], axis=1)
    mix = jnp.concatenate([top, low], axis=0).astype(jnp.bfloat16)
    return rows, mix


def unpack_result(total, count):
    half = count * NC
    out_re = total[:NV, :half] - total[NV:, half : 2 * half]
    out_im = total[NV:, :half] + total[:NV, half : 2 * half]
    out = jnp.stack([out_re, out_im]).reshape(2, NV, count, NC)
    return out.transpose(2, 0, 1, 3).reshape(count, 2 * NV * NC)


def fold_rows(f_rows, cond, count):
    t = dot_nt(f_rows, cond)
    rows, lanes = t.shape
    keep = (lax.broadcasted_iota(jnp.int32, t.shape, 0) // NV) % count == (
        lax.broadcasted_iota(jnp.int32, t.shape, 1) // NC
    ) % count
    t = jnp.where(keep, t, 0.0).reshape(2, count, NV, lanes)
    return jnp.sum(t, axis=1).reshape(2 * NV, lanes)


def per_device_general(wavefunc, haydock, screened, coulomb, umklapp_map):
    count, _, _, planes = wavefunc.shape
    blocks = lax.axis_size("blk")
    edge = count * NV
    rows, mix = make_pieces(wavefunc, haydock)
    val, cond = rows[0], rows[1]
    amp = dot_nn(mix, val)
    wide = cond.astype(jnp.float32)
    c_re, c_im, a_re, a_im = wide[:edge], wide[edge:], amp[:edge], amp[edge:]
    x_re = jnp.sum(c_re * a_re + c_im * a_im, axis=0)
    x_im = jnp.sum(c_re * a_im - c_im * a_re, axis=0)
    xs = lax.psum(jnp.stack([x_re, x_im]), "blk")
    scale_d, scale_x = scales(planes, count, count * blocks)
    y = xs * coulomb * scale_x
    v_re, v_im = val[:edge].astype(jnp.float32), val[edge:].astype(jnp.float32)
    f = jnp.concatenate([y[0] * v_re + y[1] * v_im, y[1] * v_re - y[0] * v_im], axis=0)
    current = jnp.concatenate([amp.astype(jnp.bfloat16), cond], axis=0)
    for stop in range(STOPS + 1):
        if stop > 0:
            current = lax.ppermute(current, "blk", [(i, (i + 1) % blocks) for i in range(blocks)])
        held = lax.axis_index("blk") == stop
        weight = lax.psum(jnp.where(held, screened[0], jnp.zeros_like(screened[0])), "blk")
        pick = (umklapp_map[stop][:, None] == jnp.arange(planes)[None, :]).astype(jnp.bfloat16)
        perm = dot_nt(current, pick).astype(jnp.bfloat16)
        amp_p, cond_t = perm[: 2 * edge], perm[2 * edge :].T
        turned = jnp.concatenate([amp_p[edge:], -amp_p[:edge]], axis=0)
        h_re = (dot_nn(cond_t, amp_p) * weight.astype(jnp.float32)).astype(jnp.bfloat16)
        h_im = (dot_nn(cond_t, turned) * weight.astype(jnp.float32)).astype(jnp.bfloat16)
        g_re, g_im = dot_nt(val, h_re), dot_nt(val, h_im)
        f = f + scale_d * jnp.concatenate([g_re[:edge] + g_im[edge:], g_im[:edge] - g_re[edge:]], axis=0)
    return unpack_result(fold_rows(f.astype(jnp.bfloat16), cond, count), count)


def solution(mesh):
    placed = (
        P(("grp", "blk"), None, None, None),
        P(("grp", "blk"), None),
        P(("grp", "blk"), None, None),
        P("grp"),
        P(),
    )
    body = per_device if mesh.shape["blk"] == 8 and mesh.shape["pair"] == 2 else per_device_general
    return jax.shard_map(
        body, mesh=mesh, in_specs=placed, out_specs=P(("grp", "blk"), None), check_vma=False
    )
```

```python
import functools
import math

import jax
import jax.numpy as jnp
from jax import lax
from jax.experimental import pallas as pl
from jax.experimental.pallas import tpu as pltpu
from jax.sharding import PartitionSpec as P

NV = 8
NC = 8
STOPS = 2
MESH = pl.DeviceIdType.MESH
NT = (((1,), (1,)), ((), ()))

OWN = {
    0: ((1, 0), (1, 1), (2, 0)),
    1: ((0, 1), (2, 1)),
    2: ((0, 0),),
    3: ((1, 0), (2, 1)),
    4: ((2, 0),),
    5: ((3, 0),),
    6: ((2, 0),),
    7: ((3, 1),),
}
ROUTE = {(3, 0): (5, ((1, 1), (2, 1))), (3, 1): (7, ((1, 1), (2, 1)))}
UNITS = {
    (0, 0): ((0, ()), (2, ((2, (1, 0)),)), (4, ((4, (1, 1)),)), (6, ((6, (1, 1)),))),
    (0, 1): ((1, ((1, None),)), (3, ((3, None),)), (5, ((5, None),)), (7, ((7, None),))),
    (1, 0): ((0, ((0, None),)), (1, ((3, (0, 1)), (2, None))), (2, ()), (3, ((4, None),))),
    (1, 1): ((7, ((0, None), (5, (0, 1)), (7, (0, 1)))), (4, ((4, (1, 0)),)), (5, ((6, None),)), (6, ())),
    (2, 0): ((0, ((0, None),)), (2, ((4, (0, 0)),)), (6, ((6, (0, 0)),)), (4, ())),
    (2, 1): ((1, ((1, None), (3, None))), (3, ((5, None),)), (7, ((7, None),)), (5, ())),
}
HUB = (0, 1)
ACTIONS = 3
CHUNKS = 2


def edges():
    to = {}
    for blk, targets in OWN.items():
        for target in targets:
            for core in range(2):
                to.setdefault(target, set()).add((blk, core))
    for worker, units in UNITS.items():
        for _, actions in units:
            for _, target in actions:
                if target is not None:
                    to.setdefault(target, set()).add(worker)
    for router, (_, targets) in ROUTE.items():
        for target in targets:
            to.setdefault(target, set()).add(router)
    for blk in range(8):
        for core in range(2):
            if (blk, core) != HUB:
                to.setdefault(HUB, set()).add((blk, core))
    for blk in range(STOPS + 1):
        to.setdefault((blk, 1), set()).add((blk, 0))
    return to


def dot_nt(a, b):
    return lax.dot_general(a, b, NT, preferred_element_type=jnp.float32)


def dot_nn(a, b):
    return jnp.dot(a, b, preferred_element_type=jnp.float32)


def lut(index, values):
    out = jnp.int32(0)
    for n, value in enumerate(values):
        if value:
            out = jnp.where(index == n, jnp.int32(value), out)
    return out


def iota(shape, dim):
    return lax.broadcasted_iota(jnp.int32, shape, dim)


def spread_matrix(edge):
    half = edge
    row, col = iota((128, 256), 0), iota((128, 256), 1)
    lane = col % 128
    y = (lane >= half).astype(jnp.int32)
    part = jnp.where(col >= 128, 1 - y, y)
    return ((row // 64 == part) & ((row % 64) // NC == lane % NV)).astype(jnp.bfloat16)


def make_mix(hay, spread, count):
    edge = count * NV
    tall = jnp.concatenate(
        [jnp.broadcast_to(hay[k : k + 1, :], (NC, 128)) for _ in range(2) for k in range(count)], axis=0
    )
    shape = (2 * edge, 128)
    row, col = iota(shape, 0), iota(shape, 1)
    tall = jnp.where(row % NC == col % NC, tall, 0.0).astype(jnp.bfloat16)
    q = dot_nn(tall, spread)
    top = row < edge
    k_row = jnp.where(top, row, row - edge) // NC
    k_col = jnp.where(col < edge, col, col - edge) // NV
    mix = jnp.where(top, jnp.where(col < edge, q[:, :128], -q[:, :128]), q[:, 128:])
    keep = (k_row == k_col) & (col < 2 * edge)
    return jnp.where(keep, mix, 0.0).astype(jnp.bfloat16)[:, : 2 * edge]


def fold_block(t, count):
    edge = count * NV
    row, col = iota(t.shape, 0), iota(t.shape, 1)
    k_row = jnp.where(row < edge, row, row - edge) // NC
    k_col = jnp.where(col < edge, col, col - edge) // NV
    t = jnp.where(k_row == k_col, t, 0.0)
    halves = []
    for x in range(2):
        acc = t[x * edge : x * edge + NC]
        for k in range(1, count):
            acc = acc + t[x * edge + k * NC : x * edge + (k + 1) * NC]
        halves.append(acc)
    return jnp.concatenate(halves, axis=0)


def lay_out(total, count):
    edge = count * NV
    z0 = jnp.concatenate([total[:NC]] * 16, axis=0)
    z1 = jnp.concatenate([total[NC:]] * 16, axis=0)
    shape = z0.shape
    row, col = iota(shape, 0), iota(shape, 1)
    y0 = col < edge
    z = jnp.where(row < 64, jnp.where(y0, z0, -z1), jnp.where(y0, z1, z0))
    z = jnp.where((row % 64) // NC == col % NV, z, 0.0)
    high = z.astype(jnp.bfloat16)
    low = (z - high.astype(jnp.float32)).astype(jnp.bfloat16)
    krow, kcol = iota((8, shape[1]), 0), iota((8, shape[1]), 1)
    pick = (jnp.where(kcol < edge, kcol, kcol - edge) // NV == krow).astype(jnp.bfloat16)
    return dot_nt(pick, high) + dot_nt(pick, low)


def kernel(
    count, scale_d, scale_x,
    piece_ref, hay_ref, weight_ref, map_ref, coul_ref, out_ref,
    pbuf, hbuf, wbuf, mbuf, coul, sel, fbuf, spread, stage, res, xbuf, ybuf,
    load_sem, recv_sem, recv_hay, send_sem, send_hay, send_res, recv_res, send_x, recv_x, send_y, recv_y,
):
    grp = lax.axis_index("grp")
    me = lax.axis_index("blk")
    p = lax.axis_index("pair")
    blocks = lax.axis_size("blk")
    dev = me * 2 + p
    planes = weight_ref.shape[1]
    edge = count * NV
    hub = HUB[0] * 2 + HUB[1]
    worker = me < STOPS + 1
    chunk = 2 * edge // CHUNKS

    def each(n, body):
        def wrapped(i, carry):
            body(i)
            return carry

        lax.fori_loop(0, n, wrapped, 0)

    barrier = pltpu.get_barrier_semaphore()
    to = edges()
    expect = [0] * 16
    masks = [0] * 16
    for (blk, core), senders in to.items():
        for sender in senders:
            expect[sender[0] * 2 + sender[1]] += 1
            masks[sender[0] * 2 + sender[1]] |= 1 << (blk * 2 + core)

    def greet(other):
        mask = lut(other, masks)
        power = lut(dev, [1 << d for d in range(8)])

        @pl.when((power > 0) & (mask // jnp.maximum(power, 1) % 2 == 1))
        def _():
            pl.semaphore_signal(barrier, inc=1, device_id=(grp, other // 2, other % 2), device_id_type=MESH)

    each(16, greet)

    loads = [
        pltpu.make_async_copy(src, dst, load_sem.at[n])
        for n, (src, dst) in enumerate(
            (
                (hay_ref, hbuf.at[me, pl.ds(0, count)]),
                (piece_ref, pbuf.at[me]),
                (map_ref, mbuf),
                (coul_ref, coul),
                (weight_ref.at[0], wbuf),
            )
        )
    ]
    for load in loads[:4]:
        load.start()

    @pl.when(worker)
    def _():
        loads[4].start()

    pl.semaphore_wait(barrier, lut(dev, expect))

    def rows_at(c):
        return pl.ds(pl.multiple_of(c * chunk, chunk), chunk)

    def hay_at(b):
        return hbuf.at[b, pl.ds(0, count)]

    def remote(src, dst, send, recv, target):
        return pltpu.make_async_remote_copy(
            src_ref=src, dst_ref=dst, send_sem=send, recv_sem=recv,
            device_id=(grp, target // 2, target % 2), device_id_type=MESH,
        )

    def drained(n, most, ref_of, sem):
        for m in range(1, most + 1):
            @pl.when(n == m)
            def _():
                pltpu.make_async_copy(ref_of(m), ref_of(m), sem).wait()

    own_targets = [0] * 24
    for m, targets in OWN.items():
        for slot, (blk, core) in enumerate(targets):
            own_targets[m * 3 + slot] = blk * 2 + core + 1

    def own_slot(slot):
        code = lut(me * 3 + slot, own_targets)
        target = jnp.maximum(code - 1, 0)

        @pl.when(code > 0)
        def _():
            @pl.when(p == 0)
            def _():
                remote(hay_ref, hay_at(me), send_hay.at[0], recv_hay.at[me], target).start()

            each(CHUNKS, lambda c: remote(
                piece_ref.at[p, rows_at(c)], pbuf.at[me, p, rows_at(c)],
                send_sem.at[0], recv_sem.at[me, c], target,
            ).start())

    each(3, own_slot)

    spread[...] = spread_matrix(edge)
    for load in loads[:4]:
        load.wait()
    mix = make_mix(hbuf[me, :count], spread[...], count)
    amp = dot_nn(mix, pbuf[me, 0])
    cond_own = pbuf[me, 1].astype(jnp.float32)
    c_re, c_im = cond_own[:edge], cond_own[edge:]
    a_re, a_im = amp[:edge], amp[edge:]
    xbuf[dev, 0:1, :] = jnp.sum(c_re * a_re + c_im * a_im, axis=0, keepdims=True)
    xbuf[dev, 1:2, :] = jnp.sum(c_re * a_im - c_im * a_re, axis=0, keepdims=True)
    x_copy = remote(xbuf.at[dev], xbuf.at[dev], send_x, recv_x, jnp.int32(hub))

    def others(body):
        def guarded(d):
            @pl.when(d != hub)
            def _():
                body(d)

        each(16, guarded)

    def y_copy(other):
        return remote(ybuf, ybuf, send_y, recv_y, other)

    @pl.when(dev != hub)
    def _():
        x_copy.start()

    def arrive(b, pass_on):
        pltpu.make_async_copy(hay_at(b), hay_at(b), recv_hay.at[b]).wait()
        pass_on(lambda target: remote(hay_at(b), hay_at(b), send_hay.at[1], recv_hay.at[b], target).start())

        def per_chunk(c):
            ref = pbuf.at[b, :, rows_at(c)]
            pltpu.make_async_copy(ref, ref, recv_sem.at[b, c]).wait()
            pass_on(lambda target: remote(ref, ref, send_sem.at[1], recv_sem.at[b, c], target).start())

        each(CHUNKS, per_chunk)

    def res_copy(t, b, core):
        return remote(stage.at[t], res.at[me], send_res, recv_res, b * 2 + core)

    partners = [0] * 24
    codes = [0] * (24 * ACTIONS)
    for (s, core), units in UNITS.items():
        for t, (i, actions) in enumerate(units):
            at = (s * 2 + core) * 4 + t
            partners[at] = i
            for n, (b, target) in enumerate(actions):
                onward = 0 if target is None else target[0] * 2 + target[1] + 1
                codes[at * ACTIONS + n] = 1 + b + 8 * onward

    def unit_of(t):
        i = lut(dev * 4 + t, partners)
        return i, (i + me) % blocks

    def action_of(t, n):
        code = lut((dev * 4 + t) * ACTIONS + n, codes)
        packed = jnp.maximum(code - 1, 0)
        onward = packed // 8
        return code > 0, packed % 8, onward > 0, jnp.maximum(onward - 1, 0)

    fifteen = xbuf.at[pl.ds(0, 15)]

    @pl.when(worker)
    def _():
        sel[...] = jnp.where(
            mbuf[pl.ds(me, 1), :] == iota((planes, planes), 0), 1.0, 0.0
        ).astype(jnp.bfloat16)
        loads[4].wait()

        def step(t):
            @pl.when((dev == hub) & (t == 1))
            def _():
                pltpu.make_async_copy(fifteen, fifteen, recv_x).wait()
                coul_row = jnp.concatenate([coul[n : n + 1, :] for n in range(planes // 128)], axis=1)
                ybuf[...] = jnp.sum(xbuf[...], axis=0) * coul_row * (0.5 * scale_x)
                others(lambda d: y_copy(d).start())

            def act(n):
                go, b, onward, target = action_of(t, n)

                def pass_on(start):
                    @pl.when(onward)
                    def _():
                        start(target)

                @pl.when(go)
                def _():
                    arrive(b, pass_on)

            each(ACTIONS, act)
            i, b = unit_of(t)
            mix_i = make_mix(hbuf[i, :count], spread[...], count)
            amp_i = dot_nn(mix_i, pbuf[i, 0]).astype(jnp.bfloat16)
            perm = dot_nn(jnp.concatenate([amp_i, pbuf[i, 1]], axis=0), sel[...])
            cond_t = perm[2 * edge :].T.astype(jnp.bfloat16)
            turned = jnp.concatenate([perm[edge : 2 * edge], -perm[:edge]], axis=0)
            both = jnp.concatenate([perm[: 2 * edge], turned], axis=1).astype(jnp.bfloat16)
            val_b = pbuf[b, 0]
            swapped = jnp.concatenate([-val_b[edge:], val_b[:edge]], axis=0)
            v_lanes = jnp.concatenate(
                [
                    jnp.concatenate([val_b[:edge], swapped[:edge]], axis=0),
                    jnp.concatenate([val_b[edge:], swapped[edge:]], axis=0),
                ],
                axis=1,
            )
            tile = 256
            for r in range(planes // tile):
                rows = slice(r * tile, (r + 1) * tile)
                w = wbuf[rows, :].astype(jnp.float32)
                h = (dot_nn(cond_t[rows], both) * jnp.concatenate([w, w], axis=1)).astype(jnp.bfloat16)
                fbuf[rows, :] = dot_nt(h, v_lanes).astype(jnp.bfloat16)
            part = fold_block(dot_nn(pbuf[b, 1], fbuf[...]), count) * scale_d
            stage[t, :, : 2 * edge] = part

            @pl.when((b == me) & (p == 0))
            def _():
                res[me, :, : 2 * edge] = part


            def send_result(core):
                @pl.when(jnp.logical_not((b == me) & (p == core)))
                def _():
                    res_copy(t, b, core).start()

            each(2, send_result)

        each(4, step)

    routed = 5 + 2 * p

    @pl.when(me == 3)
    def _():
        arrive(routed, lambda start: each(2, lambda slot: start(3 + 2 * slot)))

    @pl.when(dev != hub)
    def _():
        pltpu.make_async_copy(ybuf, ybuf, recv_y).wait()

    y_re, y_im = ybuf[0:1, :], ybuf[1:2, :]
    v_re = pbuf[me, 0, :edge].astype(jnp.float32)
    v_im = pbuf[me, 0, edge:].astype(jnp.float32)
    f_rows = jnp.concatenate([y_re * v_re + y_im * v_im, y_im * v_re - y_re * v_im], axis=0)
    total = fold_block(dot_nt(pbuf[me, 1], f_rows.astype(jnp.bfloat16)), count)

    awaited = jnp.where((p == 0) & worker, STOPS, STOPS + 1)
    drained(awaited, STOPS + 1, lambda n: res.at[pl.ds(0, n)], recv_res)
    for s in range(STOPS + 1):
        total = total + res[s, :, : 2 * edge]
    out_ref[...] = lay_out(total, count)[:count]

    own_count = lut(me, [len(OWN[m]) for m in range(8)])
    drained(own_count, 3, lambda n: pbuf.at[pl.ds(0, n), 0], send_sem.at[0])
    drained(jnp.where(p == 0, own_count, 0), 3, lambda n: hbuf.at[pl.ds(0, n), pl.ds(0, count)], send_hay.at[0])
    passed = [0] * 16
    for (s, core), units in UNITS.items():
        passed[s * 2 + core] = sum(target is not None for _, actions in units for _, target in actions)
    for (blk, core), (_, targets) in ROUTE.items():
        passed[blk * 2 + core] = len(targets)
    passed = lut(dev, passed)
    drained(passed, 3, lambda n: pbuf.at[pl.ds(0, n)], send_sem.at[1])
    drained(passed, 3, lambda n: hbuf.at[pl.ds(0, n), pl.ds(0, count)], send_hay.at[1])

    @pl.when(dev != hub)
    def _():
        x_copy.wait_send()

    @pl.when(dev == hub)
    def _():
        pltpu.make_async_copy(fifteen, fifteen, send_y).wait()

    for n in (7, 8):
        @pl.when(worker & (8 - n == 1 - p))
        def _():
            pltpu.make_async_copy(stage.at[pl.ds(0, n)], stage.at[pl.ds(0, n)], send_res).wait()


def scales(planes, count, total_k):
    return (
        -1.0 / (8.0 * math.sqrt(planes * count * (STOPS + 1))),
        1.0 / (8.0 * math.sqrt(planes * total_k)),
    )


def rows_of(wave):
    count, _, _, planes = wave.shape
    rows = wave.reshape(count, 2, NV, 2, planes).transpose(1, 3, 0, 2, 4)
    return rows.reshape(2, 2 * count * NV, planes)


def per_device(wavefunc, haydock, screened, coulomb, umklapp_map):
    count, _, _, planes = wavefunc.shape
    blocks = lax.axis_size("blk")
    edge = count * NV
    scale_d, scale_x = scales(planes, count, count * blocks)
    dma = pltpu.SemaphoreType.DMA
    return pl.pallas_call(
        functools.partial(kernel, count, scale_d, scale_x),
        out_shape=jax.ShapeDtypeStruct((count, 128), jnp.float32),
        in_specs=[pl.BlockSpec(memory_space=pltpu.HBM)] * 5,
        out_specs=pl.BlockSpec(memory_space=pltpu.VMEM),
        scratch_shapes=[
            pltpu.VMEM((blocks, 2, 2 * edge, planes), jnp.bfloat16),
            pltpu.VMEM((blocks, 8, 128), jnp.float32),
            pltpu.VMEM((planes, planes), jnp.bfloat16),
            pltpu.VMEM((STOPS + 1, planes), jnp.int32),
            pltpu.VMEM((planes // 128, 128), jnp.float32),
            pltpu.VMEM((planes, planes), jnp.bfloat16),
            pltpu.VMEM((planes, 2 * edge), jnp.bfloat16),
            pltpu.VMEM((128, 256), jnp.bfloat16),
            pltpu.VMEM((8, 2 * NV, 128), jnp.float32),
            pltpu.VMEM((STOPS + 1, 2 * NV, 128), jnp.float32),
            pltpu.VMEM((2 * blocks, 2, planes), jnp.float32),
            pltpu.VMEM((2, planes), jnp.float32),
            dma((5,)),
            dma((blocks, CHUNKS)),
            dma((blocks,)),
            dma((2,)),
            dma((2,)),
            dma,
            dma,
            dma,
            dma,
            dma,
            dma,
        ],
        compiler_params=pltpu.CompilerParams(
            collective_id=0, has_side_effects=True, vmem_limit_bytes=62 * 1024 * 1024
        ),
    )(rows_of(wavefunc), haydock, screened, umklapp_map, coulomb.reshape(-1, 128))


def make_pieces(wave, hay):
    count, bands, _, planes = wave.shape
    rows = wave.reshape(count, 2, NV, 2, planes).transpose(1, 3, 0, 2, 4)
    rows = rows.reshape(2, 2 * count * NV, planes)
    psi = hay.reshape(count, 2, NV, NC).transpose(1, 0, 3, 2)
    eye = jnp.eye(count, dtype=jnp.float32)
    wide = (psi[:, :, :, None, :] * eye[None, :, None, :, None]).reshape(2, count * NC, count * NV)
    top = jnp.concatenate([wide[0], -wide[1]], axis=1)
    low = jnp.concatenate([wide[1], wide[0]], axis=1)
    mix = jnp.concatenate([top, low], axis=0).astype(jnp.bfloat16)
    return rows, mix


def unpack_result(total, count):
    half = count * NC
    out_re = total[:NV, :half] - total[NV:, half : 2 * half]
    out_im = total[NV:, :half] + total[:NV, half : 2 * half]
    out = jnp.stack([out_re, out_im]).reshape(2, NV, count, NC)
    return out.transpose(2, 0, 1, 3).reshape(count, 2 * NV * NC)


def fold_rows(f_rows, cond, count):
    t = dot_nt(f_rows, cond)
    rows, lanes = t.shape
    keep = (lax.broadcasted_iota(jnp.int32, t.shape, 0) // NV) % count == (
        lax.broadcasted_iota(jnp.int32, t.shape, 1) // NC
    ) % count
    t = jnp.where(keep, t, 0.0).reshape(2, count, NV, lanes)
    return jnp.sum(t, axis=1).reshape(2 * NV, lanes)


def per_device_general(wavefunc, haydock, screened, coulomb, umklapp_map):
    count, _, _, planes = wavefunc.shape
    blocks = lax.axis_size("blk")
    edge = count * NV
    rows, mix = make_pieces(wavefunc, haydock)
    val, cond = rows[0], rows[1]
    amp = dot_nn(mix, val)
    wide = cond.astype(jnp.float32)
    c_re, c_im, a_re, a_im = wide[:edge], wide[edge:], amp[:edge], amp[edge:]
    x_re = jnp.sum(c_re * a_re + c_im * a_im, axis=0)
    x_im = jnp.sum(c_re * a_im - c_im * a_re, axis=0)
    xs = lax.psum(jnp.stack([x_re, x_im]), "blk")
    scale_d, scale_x = scales(planes, count, count * blocks)
    y = xs * coulomb * scale_x
    v_re, v_im = val[:edge].astype(jnp.float32), val[edge:].astype(jnp.float32)
    f = jnp.concatenate([y[0] * v_re + y[1] * v_im, y[1] * v_re - y[0] * v_im], axis=0)
    current = jnp.concatenate([amp.astype(jnp.bfloat16), cond], axis=0)
    for stop in range(STOPS + 1):
        if stop > 0:
            current = lax.ppermute(current, "blk", [(i, (i + 1) % blocks) for i in range(blocks)])
        held = lax.axis_index("blk") == stop
        weight = lax.psum(jnp.where(held, screened[0], jnp.zeros_like(screened[0])), "blk")
        pick = (umklapp_map[stop][:, None] == jnp.arange(planes)[None, :]).astype(jnp.bfloat16)
        perm = dot_nt(current, pick).astype(jnp.bfloat16)
        amp_p, cond_t = perm[: 2 * edge], perm[2 * edge :].T
        turned = jnp.concatenate([amp_p[edge:], -amp_p[:edge]], axis=0)
        h_re = (dot_nn(cond_t, amp_p) * weight.astype(jnp.float32)).astype(jnp.bfloat16)
        h_im = (dot_nn(cond_t, turned) * weight.astype(jnp.float32)).astype(jnp.bfloat16)
        g_re, g_im = dot_nt(val, h_re), dot_nt(val, h_im)
        f = f + scale_d * jnp.concatenate([g_re[:edge] + g_im[edge:], g_im[:edge] - g_re[edge:]], axis=0)
    return unpack_result(fold_rows(f.astype(jnp.bfloat16), cond, count), count)


def solution(mesh):
    placed = (
        P(("grp", "blk"), None, None, None),
        P(("grp", "blk"), None),
        P(("grp", "blk"), None, None),
        P("grp"),
        P(),
    )
    body = per_device if mesh.shape["blk"] == 8 and mesh.shape["pair"] == 2 else per_device_general
    return jax.shard_map(
        body, mesh=mesh, in_specs=placed, out_specs=P(("grp", "blk"), None), check_vma=False
    )
```

```python
import functools
import math

import jax
import jax.numpy as jnp
from jax import lax
from jax.experimental import pallas as pl
from jax.experimental.pallas import tpu as pltpu
from jax.sharding import PartitionSpec as P

NV = 8
NC = 8
STOPS = 2
MESH = pl.DeviceIdType.MESH
NT = (((1,), (1,)), ((), ()))

OWN = {
    0: ((1, 0), (2, 0)),
    1: ((0, 1),),
    2: ((0, 0),),
    3: ((1, 1), (2, 1)),
    4: ((2, 0),),
    5: ((3, 0),),
    6: ((2, 0),),
    7: ((3, 1),),
}
UNITS = {
    (0, 0): ((0, ()), (2, ((2, ((1, 1),)),)), (4, ((4, ()),)), (6, ((6, ()),))),
    (0, 1): ((1, ((1, ((2, 1),)),)), (3, ((3, ()),)), (5, ((5, ()),)), (7, ((7, ()),))),
    (1, 0): ((0, ((0, ()),)), (7, ((7, ((0, 1),)),))),
    (1, 1): ((1, ((3, ((0, 1),)), (2, ()))), (2, ())),
    (2, 0): (
        (0, ((0, ()),)),
        (2, ((4, ((0, 0), (3, 0))),)),
        (6, ((6, ((0, 0), (3, 1))),)),
        (4, ()),
    ),
    (2, 1): ((1, ((3, ()), (1, ()))), (3, ((5, ()),)), (7, ((7, ()),)), (5, ())),
    (3, 0): ((3, ((5, ((2, 1), (0, 1), (3, 1))), (4, ()))), (4, ())),
    (3, 1): ((5, ((7, ((1, 0), (2, 1))), (5, ()), (6, ()))), (6, ())),
}
LENT = 1
LENT_TO = 3
WCHUNKS = 3
HUB = (0, 1)
ACTIONS = 3
CHUNKS = 2


def edges():
    to = {}
    for blk, targets in OWN.items():
        for target in targets:
            for core in range(2):
                to.setdefault(target, set()).add((blk, core))
    for worker, units in UNITS.items():
        for _, actions in units:
            for _, targets in actions:
                for target in targets:
                    to.setdefault(target, set()).add(worker)
    for core in range(2):
        to.setdefault((LENT_TO, core), set()).update({(LENT, core), (LENT_TO, 1 - core)})
    for blk in range(8):
        for core in range(2):
            if (blk, core) != HUB:
                to.setdefault(HUB, set()).add((blk, core))
    for blk in range(STOPS + 1):
        to.setdefault((blk, 1), set()).add((blk, 0))
    return to


def dot_nt(a, b):
    return lax.dot_general(a, b, NT, preferred_element_type=jnp.float32)


def dot_nn(a, b):
    return jnp.dot(a, b, preferred_element_type=jnp.float32)


def lut(index, values):
    out = jnp.int32(0)
    for n, value in enumerate(values):
        if value:
            out = jnp.where(index == n, jnp.int32(value), out)
    return out


def iota(shape, dim):
    return lax.broadcasted_iota(jnp.int32, shape, dim)


def spread_matrix(edge):
    half = edge
    row, col = iota((128, 256), 0), iota((128, 256), 1)
    lane = col % 128
    y = (lane >= half).astype(jnp.int32)
    part = jnp.where(col >= 128, 1 - y, y)
    return ((row // 64 == part) & ((row % 64) // NC == lane % NV)).astype(jnp.bfloat16)


def make_mix(hay, spread, count):
    edge = count * NV
    tall = jnp.concatenate(
        [jnp.broadcast_to(hay[k : k + 1, :], (NC, 128)) for _ in range(2) for k in range(count)], axis=0
    )
    shape = (2 * edge, 128)
    row, col = iota(shape, 0), iota(shape, 1)
    tall = jnp.where(row % NC == col % NC, tall, 0.0).astype(jnp.bfloat16)
    q = dot_nn(tall, spread)
    top = row < edge
    k_row = jnp.where(top, row, row - edge) // NC
    k_col = jnp.where(col < edge, col, col - edge) // NV
    mix = jnp.where(top, jnp.where(col < edge, q[:, :128], -q[:, :128]), q[:, 128:])
    keep = (k_row == k_col) & (col < 2 * edge)
    return jnp.where(keep, mix, 0.0).astype(jnp.bfloat16)[:, : 2 * edge]


def fold_block(t, count):
    edge = count * NV
    row, col = iota(t.shape, 0), iota(t.shape, 1)
    k_row = jnp.where(row < edge, row, row - edge) // NC
    k_col = jnp.where(col < edge, col, col - edge) // NV
    t = jnp.where(k_row == k_col, t, 0.0)
    halves = []
    for x in range(2):
        acc = t[x * edge : x * edge + NC]
        for k in range(1, count):
            acc = acc + t[x * edge + k * NC : x * edge + (k + 1) * NC]
        halves.append(acc)
    return jnp.concatenate(halves, axis=0)


def lay_out(total, count):
    edge = count * NV
    z0 = jnp.concatenate([total[:NC]] * 16, axis=0)
    z1 = jnp.concatenate([total[NC:]] * 16, axis=0)
    shape = z0.shape
    row, col = iota(shape, 0), iota(shape, 1)
    y0 = col < edge
    z = jnp.where(row < 64, jnp.where(y0, z0, -z1), jnp.where(y0, z1, z0))
    z = jnp.where((row % 64) // NC == col % NV, z, 0.0)
    high = z.astype(jnp.bfloat16)
    low = (z - high.astype(jnp.float32)).astype(jnp.bfloat16)
    krow, kcol = iota((8, shape[1]), 0), iota((8, shape[1]), 1)
    pick = (jnp.where(kcol < edge, kcol, kcol - edge) // NV == krow).astype(jnp.bfloat16)
    return dot_nt(pick, high) + dot_nt(pick, low)


def kernel(
    count, scale_d, scale_x,
    piece_ref, hay_ref, weight_ref, map_ref, coul_ref, out_ref,
    pbuf, hbuf, wbuf, mbuf, coul, sel, fbuf, spread, stage, res, xbuf, ybuf,
    load_sem, recv_sem, recv_hay, recv_w, send_w, send_sem, send_hay, send_res, recv_res, send_x, recv_x, send_y, recv_y,
):
    grp = lax.axis_index("grp")
    me = lax.axis_index("blk")
    p = lax.axis_index("pair")
    blocks = lax.axis_size("blk")
    dev = me * 2 + p
    planes = weight_ref.shape[1]
    edge = count * NV
    hub = HUB[0] * 2 + HUB[1]
    holder = me < STOPS + 1
    worker = holder | (me == LENT_TO)
    stop = jnp.where(me == LENT_TO, LENT, me)
    chunk = 2 * edge // CHUNKS

    def each(n, body):
        def wrapped(i, carry):
            body(i)
            return carry

        lax.fori_loop(0, n, wrapped, 0)

    barrier = pltpu.get_barrier_semaphore()
    to = edges()
    expect = [0] * 16
    masks = [0] * 16
    for (blk, core), senders in to.items():
        for sender in senders:
            expect[sender[0] * 2 + sender[1]] += 1
            masks[sender[0] * 2 + sender[1]] |= 1 << (blk * 2 + core)

    def greet(other):
        mask = lut(other, masks)
        power = lut(dev, [1 << d for d in range(8)])

        @pl.when((power > 0) & (mask // jnp.maximum(power, 1) % 2 == 1))
        def _():
            pl.semaphore_signal(barrier, inc=1, device_id=(grp, other // 2, other % 2), device_id_type=MESH)

    each(16, greet)

    loads = [
        pltpu.make_async_copy(src, dst, load_sem.at[n])
        for n, (src, dst) in enumerate(
            (
                (hay_ref, hbuf.at[me, pl.ds(0, count)]),
                (piece_ref, pbuf.at[me]),
                (map_ref, mbuf),
                (coul_ref, coul),
                (weight_ref.at[0], wbuf),
            )
        )
    ]
    for load in loads[:4]:
        load.start()

    @pl.when(holder)
    def _():
        loads[4].start()

    pl.semaphore_wait(barrier, lut(dev, expect))

    def rows_at(c):
        return pl.ds(pl.multiple_of(c * chunk, chunk), chunk)

    def hay_at(b):
        return hbuf.at[b, pl.ds(0, count)]

    def remote(src, dst, send, recv, target):
        return pltpu.make_async_remote_copy(
            src_ref=src, dst_ref=dst, send_sem=send, recv_sem=recv,
            device_id=(grp, target // 2, target % 2), device_id_type=MESH,
        )

    def drained(n, most, ref_of, sem):
        for m in range(1, most + 1):
            @pl.when(n == m)
            def _():
                pltpu.make_async_copy(ref_of(m), ref_of(m), sem).wait()

    own_targets = [0] * 24
    for m, targets in OWN.items():
        for slot, (blk, core) in enumerate(targets):
            own_targets[m * 3 + slot] = blk * 2 + core + 1

    def own_slot(slot):
        code = lut(me * 3 + slot, own_targets)
        target = jnp.maximum(code - 1, 0)

        @pl.when(code > 0)
        def _():
            @pl.when(p == 0)
            def _():
                remote(hay_ref, hay_at(me), send_hay.at[0], recv_hay.at[me], target).start()

            each(CHUNKS, lambda c: remote(
                piece_ref.at[p, rows_at(c)], pbuf.at[me, p, rows_at(c)],
                send_sem.at[0], recv_sem.at[me, c], target,
            ).start())

    each(3, own_slot)
    half = planes // 2
    share = half // WCHUNKS

    def lent_rows(core, c):
        return pl.ds(pl.multiple_of(core * half + c * share, share), share)

    @pl.when(me == LENT)
    def _():
        each(WCHUNKS, lambda c: remote(
            weight_ref.at[0, lent_rows(p, c)], wbuf.at[lent_rows(p, c)],
            send_w, recv_w.at[p, c], LENT_TO * 2 + p,
        ).start())

    def take_lent():
        def own_half(c):
            ref = wbuf.at[lent_rows(p, c)]
            pltpu.make_async_copy(ref, ref, recv_w.at[p, c]).wait()
            remote(ref, ref, send_w, recv_w.at[p, c], LENT_TO * 2 + 1 - p).start()

        def other_half(c):
            ref = wbuf.at[lent_rows(1 - p, c)]
            pltpu.make_async_copy(ref, ref, recv_w.at[1 - p, c]).wait()

        each(WCHUNKS, own_half)
        each(WCHUNKS, other_half)


    spread[...] = spread_matrix(edge)
    for load in loads[:4]:
        load.wait()
    mix = make_mix(hbuf[me, :count], spread[...], count)
    amp = dot_nn(mix, pbuf[me, 0])
    cond_own = pbuf[me, 1].astype(jnp.float32)
    c_re, c_im = cond_own[:edge], cond_own[edge:]
    a_re, a_im = amp[:edge], amp[edge:]
    xbuf[dev, 0:1, :] = jnp.sum(c_re * a_re + c_im * a_im, axis=0, keepdims=True)
    xbuf[dev, 1:2, :] = jnp.sum(c_re * a_im - c_im * a_re, axis=0, keepdims=True)
    x_copy = remote(xbuf.at[dev], xbuf.at[dev], send_x, recv_x, jnp.int32(hub))

    def others(body):
        def guarded(d):
            @pl.when(d != hub)
            def _():
                body(d)

        each(16, guarded)

    def y_copy(other):
        return remote(ybuf, ybuf, send_y, recv_y, other)

    @pl.when(dev != hub)
    def _():
        x_copy.start()

    def arrive(b, pass_on):
        pltpu.make_async_copy(hay_at(b), hay_at(b), recv_hay.at[b]).wait()
        pass_on(lambda target: remote(hay_at(b), hay_at(b), send_hay.at[1], recv_hay.at[b], target).start())

        def per_chunk(c):
            ref = pbuf.at[b, :, rows_at(c)]
            pltpu.make_async_copy(ref, ref, recv_sem.at[b, c]).wait()
            pass_on(lambda target: remote(ref, ref, send_sem.at[1], recv_sem.at[b, c], target).start())

        each(CHUNKS, per_chunk)

    def res_copy(t, b, core):
        return remote(stage.at[t], res.at[stop], send_res, recv_res, b * 2 + core)

    partners = [0] * 32
    codes = [0] * (32 * ACTIONS)
    passed = [0] * 16
    results = [0] * 16
    for (blk, core), units in UNITS.items():
        d = blk * 2 + core
        results[d] = 2 * len(units) - (blk <= STOPS and core == 0)
        for t, (i, actions) in enumerate(units):
            partners[d * 4 + t] = i + 1
            for n, (b, targets) in enumerate(actions):
                code = 0
                for target in reversed(targets):
                    code = code * 17 + target[0] * 2 + target[1] + 1
                codes[(d * 4 + t) * ACTIONS + n] = 1 + b + 8 * code
                passed[d] += len(targets)

    def unit(t, i):
        b = (i + stop) % blocks
        mix_i = make_mix(hbuf[i, :count], spread[...], count)
        amp_i = dot_nn(mix_i, pbuf[i, 0]).astype(jnp.bfloat16)
        perm = dot_nn(jnp.concatenate([amp_i, pbuf[i, 1]], axis=0), sel[...])
        cond_t = perm[2 * edge :].T.astype(jnp.bfloat16)
        turned = jnp.concatenate([perm[edge : 2 * edge], -perm[:edge]], axis=0)
        both = jnp.concatenate([perm[: 2 * edge], turned], axis=1).astype(jnp.bfloat16)
        val_b = pbuf[b, 0]
        swapped = jnp.concatenate([-val_b[edge:], val_b[:edge]], axis=0)
        v_lanes = jnp.concatenate(
            [
                jnp.concatenate([val_b[:edge], swapped[:edge]], axis=0),
                jnp.concatenate([val_b[edge:], swapped[edge:]], axis=0),
            ],
            axis=1,
        )

        @pl.when((me == LENT_TO) & (t == 0))
        def _():
            take_lent()

        tile = 256
        for r in range(planes // tile):
            rows = slice(r * tile, (r + 1) * tile)
            w = wbuf[rows, :].astype(jnp.float32)
            h = (dot_nn(cond_t[rows], both) * jnp.concatenate([w, w], axis=1)).astype(jnp.bfloat16)
            fbuf[rows, :] = dot_nt(h, v_lanes).astype(jnp.bfloat16)
        part = fold_block(dot_nn(pbuf[b, 1], fbuf[...]), count) * scale_d
        stage[t, :, : 2 * edge] = part

        @pl.when((b == me) & (p == 0))
        def _():
            res[stop, :, : 2 * edge] = part


        def send_result(core):
            @pl.when(jnp.logical_not((b == me) & (p == core)))
            def _():
                res_copy(t, b, core).start()

        each(2, send_result)


    fifteen = xbuf.at[pl.ds(0, 15)]

    @pl.when(worker)
    def _():
        sel[...] = jnp.where(
            mbuf[pl.ds(stop, 1), :] == iota((planes, planes), 0), 1.0, 0.0
        ).astype(jnp.bfloat16)

        @pl.when(holder)
        def _():
            loads[4].wait()

        def step(t):
            @pl.when((dev == hub) & (t == 1))
            def _():
                pltpu.make_async_copy(fifteen, fifteen, recv_x).wait()
                coul_row = jnp.concatenate([coul[n : n + 1, :] for n in range(planes // 128)], axis=1)
                ybuf[...] = jnp.sum(xbuf[...], axis=0) * coul_row * (0.5 * scale_x)
                others(lambda d: y_copy(d).start())

            def act(n):
                code = lut((dev * 4 + t) * ACTIONS + n, codes)
                packed = jnp.maximum(code - 1, 0)
                onward = packed // 8

                def pass_on(start):
                    def per_target(slot):
                        target = onward // lut(slot, [1, 17, 289]) % 17

                        @pl.when(target > 0)
                        def _():
                            start(jnp.maximum(target - 1, 0))

                    each(3, per_target)

                @pl.when(code > 0)
                def _():
                    arrive(packed % 8, pass_on)

            each(ACTIONS, act)
            i = lut(dev * 4 + t, partners) - 1

            @pl.when(i >= 0)
            def _():
                unit(t, jnp.maximum(i, 0))

        each(4, step)

    @pl.when(dev != hub)
    def _():
        pltpu.make_async_copy(ybuf, ybuf, recv_y).wait()

    y_re, y_im = ybuf[0:1, :], ybuf[1:2, :]
    v_re = pbuf[me, 0, :edge].astype(jnp.float32)
    v_im = pbuf[me, 0, edge:].astype(jnp.float32)
    f_rows = jnp.concatenate([y_re * v_re + y_im * v_im, y_im * v_re - y_re * v_im], axis=0)
    total = fold_block(dot_nt(pbuf[me, 1], f_rows.astype(jnp.bfloat16)), count)

    awaited = jnp.where((p == 0) & holder, STOPS, STOPS + 1)
    drained(awaited, STOPS + 1, lambda n: res.at[pl.ds(0, n)], recv_res)
    for s in range(STOPS + 1):
        total = total + res[s, :, : 2 * edge]
    out_ref[...] = lay_out(total, count)[:count]

    own_count = lut(me, [len(OWN[m]) for m in range(8)])
    drained(own_count, 3, lambda n: pbuf.at[pl.ds(0, n), 0], send_sem.at[0])
    drained(jnp.where(p == 0, own_count, 0), 3, lambda n: hbuf.at[pl.ds(0, n), pl.ds(0, count)], send_hay.at[0])
    passed = lut(dev, passed)
    drained(passed, 4, lambda n: pbuf.at[pl.ds(0, n)], send_sem.at[1])
    drained(passed, 4, lambda n: hbuf.at[pl.ds(0, n), pl.ds(0, count)], send_hay.at[1])

    @pl.when(dev != hub)
    def _():
        x_copy.wait_send()

    @pl.when(dev == hub)
    def _():
        pltpu.make_async_copy(fifteen, fifteen, send_y).wait()

    drained(lut(dev, results), 8, lambda n: stage.at[pl.ds(0, n)], send_res)

    @pl.when((me == LENT) | (me == LENT_TO))
    def _():
        pltpu.make_async_copy(wbuf.at[pl.ds(0, half)], wbuf.at[pl.ds(0, half)], send_w).wait()


def scales(planes, count, total_k):
    return (
        -1.0 / (8.0 * math.sqrt(planes * count * (STOPS + 1))),
        1.0 / (8.0 * math.sqrt(planes * total_k)),
    )


def rows_of(wave):
    count, _, _, planes = wave.shape
    rows = wave.reshape(count, 2, NV, 2, planes).transpose(1, 3, 0, 2, 4)
    return rows.reshape(2, 2 * count * NV, planes)


def per_device(wavefunc, haydock, screened, coulomb, umklapp_map):
    count, _, _, planes = wavefunc.shape
    blocks = lax.axis_size("blk")
    edge = count * NV
    scale_d, scale_x = scales(planes, count, count * blocks)
    dma = pltpu.SemaphoreType.DMA
    return pl.pallas_call(
        functools.partial(kernel, count, scale_d, scale_x),
        out_shape=jax.ShapeDtypeStruct((count, 128), jnp.float32),
        in_specs=[pl.BlockSpec(memory_space=pltpu.HBM)] * 5,
        out_specs=pl.BlockSpec(memory_space=pltpu.VMEM),
        scratch_shapes=[
            pltpu.VMEM((blocks, 2, 2 * edge, planes), jnp.bfloat16),
            pltpu.VMEM((blocks, 8, 128), jnp.float32),
            pltpu.VMEM((planes, planes), jnp.bfloat16),
            pltpu.VMEM((STOPS + 1, planes), jnp.int32),
            pltpu.VMEM((planes // 128, 128), jnp.float32),
            pltpu.VMEM((planes, planes), jnp.bfloat16),
            pltpu.VMEM((planes, 2 * edge), jnp.bfloat16),
            pltpu.VMEM((128, 256), jnp.bfloat16),
            pltpu.VMEM((8, 2 * NV, 128), jnp.float32),
            pltpu.VMEM((STOPS + 1, 2 * NV, 128), jnp.float32),
            pltpu.VMEM((2 * blocks, 2, planes), jnp.float32),
            pltpu.VMEM((2, planes), jnp.float32),
            dma((5,)),
            dma((blocks, CHUNKS)),
            dma((blocks,)),
            dma((2, WCHUNKS)),
            dma,
            dma((2,)),
            dma((2,)),
            dma,
            dma,
            dma,
            dma,
            dma,
            dma,
        ],
        compiler_params=pltpu.CompilerParams(
            collective_id=0, has_side_effects=True, vmem_limit_bytes=62 * 1024 * 1024
        ),
    )(rows_of(wavefunc), haydock, screened, umklapp_map, coulomb.reshape(-1, 128))


def make_pieces(wave, hay):
    count, bands, _, planes = wave.shape
    rows = wave.reshape(count, 2, NV, 2, planes).transpose(1, 3, 0, 2, 4)
    rows = rows.reshape(2, 2 * count * NV, planes)
    psi = hay.reshape(count, 2, NV, NC).transpose(1, 0, 3, 2)
    eye = jnp.eye(count, dtype=jnp.float32)
    wide = (psi[:, :, :, None, :] * eye[None, :, None, :, None]).reshape(2, count * NC, count * NV)
    top = jnp.concatenate([wide[0], -wide[1]], axis=1)
    low = jnp.concatenate([wide[1], wide[0]], axis=1)
    mix = jnp.concatenate([top, low], axis=0).astype(jnp.bfloat16)
    return rows, mix


def unpack_result(total, count):
    half = count * NC
    out_re = total[:NV, :half] - total[NV:, half : 2 * half]
    out_im = total[NV:, :half] + total[:NV, half : 2 * half]
    out = jnp.stack([out_re, out_im]).reshape(2, NV, count, NC)
    return out.transpose(2, 0, 1, 3).reshape(count, 2 * NV * NC)


def fold_rows(f_rows, cond, count):
    t = dot_nt(f_rows, cond)
    rows, lanes = t.shape
    keep = (lax.broadcasted_iota(jnp.int32, t.shape, 0) // NV) % count == (
        lax.broadcasted_iota(jnp.int32, t.shape, 1) // NC
    ) % count
    t = jnp.where(keep, t, 0.0).reshape(2, count, NV, lanes)
    return jnp.sum(t, axis=1).reshape(2 * NV, lanes)


def per_device_general(wavefunc, haydock, screened, coulomb, umklapp_map):
    count, _, _, planes = wavefunc.shape
    blocks = lax.axis_size("blk")
    edge = count * NV
    rows, mix = make_pieces(wavefunc, haydock)
    val, cond = rows[0], rows[1]
    amp = dot_nn(mix, val)
    wide = cond.astype(jnp.float32)
    c_re, c_im, a_re, a_im = wide[:edge], wide[edge:], amp[:edge], amp[edge:]
    x_re = jnp.sum(c_re * a_re + c_im * a_im, axis=0)
    x_im = jnp.sum(c_re * a_im - c_im * a_re, axis=0)
    xs = lax.psum(jnp.stack([x_re, x_im]), "blk")
    scale_d, scale_x = scales(planes, count, count * blocks)
    y = xs * coulomb * scale_x
    v_re, v_im = val[:edge].astype(jnp.float32), val[edge:].astype(jnp.float32)
    f = jnp.concatenate([y[0] * v_re + y[1] * v_im, y[1] * v_re - y[0] * v_im], axis=0)
    current = jnp.concatenate([amp.astype(jnp.bfloat16), cond], axis=0)
    for stop in range(STOPS + 1):
        if stop > 0:
            current = lax.ppermute(current, "blk", [(i, (i + 1) % blocks) for i in range(blocks)])
        held = lax.axis_index("blk") == stop
        weight = lax.psum(jnp.where(held, screened[0], jnp.zeros_like(screened[0])), "blk")
        pick = (umklapp_map[stop][:, None] == jnp.arange(planes)[None, :]).astype(jnp.bfloat16)
        perm = dot_nt(current, pick).astype(jnp.bfloat16)
        amp_p, cond_t = perm[: 2 * edge], perm[2 * edge :].T
        turned = jnp.concatenate([amp_p[edge:], -amp_p[:edge]], axis=0)
        h_re = (dot_nn(cond_t, amp_p) * weight.astype(jnp.float32)).astype(jnp.bfloat16)
        h_im = (dot_nn(cond_t, turned) * weight.astype(jnp.float32)).astype(jnp.bfloat16)
        g_re, g_im = dot_nt(val, h_re), dot_nt(val, h_im)
        f = f + scale_d * jnp.concatenate([g_re[:edge] + g_im[edge:], g_im[:edge] - g_re[edge:]], axis=0)
    return unpack_result(fold_rows(f.astype(jnp.bfloat16), cond, count), count)


def solution(mesh):
    placed = (
        P(("grp", "blk"), None, None, None),
        P(("grp", "blk"), None),
        P(("grp", "blk"), None, None),
        P("grp"),
        P(),
    )
    body = per_device if mesh.shape["blk"] == 8 and mesh.shape["pair"] == 2 else per_device_general
    return jax.shard_map(
        body, mesh=mesh, in_specs=placed, out_specs=P(("grp", "blk"), None), check_vma=False
    )
```

```python
import functools
import math

import jax
import jax.numpy as jnp
from jax import lax
from jax.experimental import pallas as pl
from jax.experimental.pallas import tpu as pltpu
from jax.sharding import PartitionSpec as P

NV = 8
NC = 8
STOPS = 2
MESH = pl.DeviceIdType.MESH
NT = (((1,), (1,)), ((), ()))

OWN = {
    0: ((1, 0), (2, 0)),
    1: ((0, 1),),
    2: ((0, 0),),
    3: ((1, 1), (2, 1)),
    4: ((2, 0),),
    5: ((3, 0),),
    6: ((2, 0),),
    7: ((3, 1),),
}
UNITS = {
    (0, 0): (((0, 2), ((2, ((1, 1),)),)), ((4, 6), ((4, ()), (6, ())))),
    (0, 1): (((1, 3), ((1, ((2, 1),)), (3, ()))), ((5, 7), ((5, ()), (7, ())))),
    (1, 0): (((0, 7), ((0, ()), (7, ((0, 1),)))),),
    (1, 1): (((1, 2), ((3, ((0, 1),)), (2, ()))),),
    (2, 0): (((6, 4), ((4, ((0, 0), (3, 0))), (6, ((0, 0), (3, 1))), (0, ()))), ((0, 2), ())),
    (2, 1): (((7, 1), ((3, ()), (1, ()), (7, ()))), ((3, 5), ((5, ()),))),
    (3, 0): (((3, 4), ((5, ((2, 1), (0, 1), (3, 1))), (4, ()))),),
    (3, 1): (((5, 6), ((7, ((1, 0), (2, 1))), (5, ()), (6, ()))),),
}
LENT = 1
LENT_TO = 3
WCHUNKS = 3
HUB = (0, 1)
ACTIONS = 3
CHUNKS = 3


def edges():
    to = {}
    for blk, targets in OWN.items():
        for target in targets:
            for core in range(2):
                to.setdefault(target, set()).add((blk, core))
    for worker, units in UNITS.items():
        for _, actions in units:
            for _, targets in actions:
                for target in targets:
                    to.setdefault(target, set()).add(worker)
    for core in range(2):
        to.setdefault((LENT_TO, core), set()).update({(LENT, core), (LENT_TO, 1 - core)})
    for blk in range(8):
        for core in range(2):
            if (blk, core) != HUB:
                to.setdefault(HUB, set()).add((blk, core))
    for blk in range(STOPS + 1):
        to.setdefault((blk, 1), set()).add((blk, 0))
    return to


def dot_nt(a, b):
    return lax.dot_general(a, b, NT, preferred_element_type=jnp.float32)


def dot_nn(a, b):
    return jnp.dot(a, b, preferred_element_type=jnp.float32)


def lut(index, values):
    out = jnp.int32(0)
    for n, value in enumerate(values):
        if value:
            out = jnp.where(index == n, jnp.int32(value), out)
    return out


def iota(shape, dim):
    return lax.broadcasted_iota(jnp.int32, shape, dim)


def spread_matrix(edge):
    half = edge
    row, col = iota((128, 256), 0), iota((128, 256), 1)
    lane = col % 128
    y = (lane >= half).astype(jnp.int32)
    part = jnp.where(col >= 128, 1 - y, y)
    return ((row // 64 == part) & ((row % 64) // NC == lane % NV)).astype(jnp.bfloat16)


def make_mix(hay, spread, count):
    edge = count * NV
    tall = jnp.concatenate(
        [jnp.broadcast_to(hay[k : k + 1, :], (NC, 128)) for _ in range(2) for k in range(count)], axis=0
    )
    shape = (2 * edge, 128)
    row, col = iota(shape, 0), iota(shape, 1)
    tall = jnp.where(row % NC == col % NC, tall, 0.0).astype(jnp.bfloat16)
    q = dot_nn(tall, spread)
    top = row < edge
    k_row = jnp.where(top, row, row - edge) // NC
    k_col = jnp.where(col < edge, col, col - edge) // NV
    mix = jnp.where(top, jnp.where(col < edge, q[:, :128], -q[:, :128]), q[:, 128:])
    keep = (k_row == k_col) & (col < 2 * edge)
    return jnp.where(keep, mix, 0.0).astype(jnp.bfloat16)[:, : 2 * edge]


def fold_block(t, count):
    edge = count * NV
    row, col = iota(t.shape, 0), iota(t.shape, 1)
    k_row = jnp.where(row < edge, row, row - edge) // NC
    k_col = jnp.where(col < edge, col, col - edge) // NV
    t = jnp.where(k_row == k_col, t, 0.0)
    halves = []
    for x in range(2):
        acc = t[x * edge : x * edge + NC]
        for k in range(1, count):
            acc = acc + t[x * edge + k * NC : x * edge + (k + 1) * NC]
        halves.append(acc)
    return jnp.concatenate(halves, axis=0)


def lay_out(total, count):
    edge = count * NV
    z0 = jnp.concatenate([total[:NC]] * 16, axis=0)
    z1 = jnp.concatenate([total[NC:]] * 16, axis=0)
    shape = z0.shape
    row, col = iota(shape, 0), iota(shape, 1)
    y0 = col < edge
    z = jnp.where(row < 64, jnp.where(y0, z0, -z1), jnp.where(y0, z1, z0))
    z = jnp.where((row % 64) // NC == col % NV, z, 0.0)
    high = z.astype(jnp.bfloat16)
    low = (z - high.astype(jnp.float32)).astype(jnp.bfloat16)
    krow, kcol = iota((8, shape[1]), 0), iota((8, shape[1]), 1)
    pick = (jnp.where(kcol < edge, kcol, kcol - edge) // NV == krow).astype(jnp.bfloat16)
    return dot_nt(pick, high) + dot_nt(pick, low)


def kernel(
    count, scale_d, scale_x,
    piece_ref, hay_ref, weight_ref, map_ref, coul_ref, out_ref,
    pbuf, hbuf, wbuf, mbuf, coul, sel, fbuf, spread, stage, res, xbuf, ybuf,
    load_sem, recv_sem, recv_hay, recv_w, send_w, send_sem, send_hay, send_res, recv_res, send_x, recv_x, send_y, recv_y,
):
    grp = lax.axis_index("grp")
    me = lax.axis_index("blk")
    p = lax.axis_index("pair")
    blocks = lax.axis_size("blk")
    dev = me * 2 + p
    planes = weight_ref.shape[1]
    edge = count * NV
    hub = HUB[0] * 2 + HUB[1]
    holder = me < STOPS + 1
    worker = holder | (me == LENT_TO)
    stop = jnp.where(me == LENT_TO, LENT, me)
    chunk = 2 * edge // CHUNKS

    def each(n, body):
        def wrapped(i, carry):
            body(i)
            return carry

        lax.fori_loop(0, n, wrapped, 0)

    barrier = pltpu.get_barrier_semaphore()
    to = edges()
    expect = [0] * 16
    masks = [0] * 16
    for (blk, core), senders in to.items():
        for sender in senders:
            expect[sender[0] * 2 + sender[1]] += 1
            masks[sender[0] * 2 + sender[1]] |= 1 << (blk * 2 + core)

    def greet(other):
        mask = lut(other, masks)
        power = lut(dev, [1 << d for d in range(16)])

        @pl.when((power > 0) & (mask // jnp.maximum(power, 1) % 2 == 1))
        def _():
            pl.semaphore_signal(barrier, inc=1, device_id=(grp, other // 2, other % 2), device_id_type=MESH)

    each(16, greet)

    loads = [
        pltpu.make_async_copy(src, dst, load_sem.at[n])
        for n, (src, dst) in enumerate(
            (
                (hay_ref, hbuf.at[me, pl.ds(0, count)]),
                (piece_ref, pbuf.at[me]),
                (map_ref, mbuf),
                (coul_ref, coul),
                (weight_ref.at[0], wbuf),
            )
        )
    ]
    for load in loads[:4]:
        load.start()

    @pl.when(holder)
    def _():
        loads[4].start()

    pl.semaphore_wait(barrier, lut(dev, expect))

    def rows_at(c):
        return pl.ds(pl.multiple_of(c * chunk, chunk), chunk)

    def hay_at(b):
        return hbuf.at[b, pl.ds(0, count)]

    def remote(src, dst, send, recv, target):
        return pltpu.make_async_remote_copy(
            src_ref=src, dst_ref=dst, send_sem=send, recv_sem=recv,
            device_id=(grp, target // 2, target % 2), device_id_type=MESH,
        )

    def drained(n, most, ref_of, sem):
        for m in range(1, most + 1):
            @pl.when(n == m)
            def _():
                pltpu.make_async_copy(ref_of(m), ref_of(m), sem).wait()

    own_targets = [0] * 24
    for m, targets in OWN.items():
        for slot, (blk, core) in enumerate(targets):
            own_targets[m * 3 + slot] = blk * 2 + core + 1

    def own_slot(slot):
        code = lut(me * 3 + slot, own_targets)
        target = jnp.maximum(code - 1, 0)

        @pl.when(code > 0)
        def _():
            @pl.when(p == 0)
            def _():
                remote(hay_ref, hay_at(me), send_hay.at[0], recv_hay.at[me], target).start()

            each(CHUNKS, lambda c: remote(
                piece_ref.at[p, rows_at(c)], pbuf.at[me, p, rows_at(c)],
                send_sem.at[0], recv_sem.at[me, c], target,
            ).start())

    half = planes // 2
    share = half // WCHUNKS

    def lent_rows(core, c):
        return pl.ds(pl.multiple_of(core * half + c * share, share), share)

    @pl.when(me == LENT)
    def _():
        each(WCHUNKS, lambda c: remote(
            weight_ref.at[0, lent_rows(p, c)], wbuf.at[lent_rows(p, c)],
            send_w, recv_w.at[p, c], LENT_TO * 2 + p,
        ).start())

    each(3, own_slot)

    def take_own():
        def per_chunk(c):
            ref = wbuf.at[lent_rows(p, c)]
            pltpu.make_async_copy(ref, ref, recv_w.at[p, c]).wait()
            remote(ref, ref, send_w, recv_w.at[p, c], LENT_TO * 2 + 1 - p).start()

        each(WCHUNKS, per_chunk)

    def take_other():
        def per_chunk(c):
            ref = wbuf.at[lent_rows(1 - p, c)]
            pltpu.make_async_copy(ref, ref, recv_w.at[1 - p, c]).wait()

        each(WCHUNKS, per_chunk)

    spread[...] = spread_matrix(edge)
    for load in loads[:4]:
        load.wait()
    mix = make_mix(hbuf[me, :count], spread[...], count)
    amp = dot_nn(mix, pbuf[me, 0])
    cond_own = pbuf[me, 1].astype(jnp.float32)
    c_re, c_im = cond_own[:edge], cond_own[edge:]
    a_re, a_im = amp[:edge], amp[edge:]
    xbuf[dev, 0:1, :] = jnp.sum(c_re * a_re + c_im * a_im, axis=0, keepdims=True)
    xbuf[dev, 1:2, :] = jnp.sum(c_re * a_im - c_im * a_re, axis=0, keepdims=True)
    x_copy = remote(xbuf.at[dev], xbuf.at[dev], send_x, recv_x, jnp.int32(hub))

    def others(body):
        def guarded(d):
            @pl.when(d != hub)
            def _():
                body(d)

        each(16, guarded)

    def y_copy(other):
        return remote(ybuf, ybuf, send_y, recv_y, other)

    @pl.when(dev != hub)
    def _():
        x_copy.start()

    def arrive(b, pass_on):
        pltpu.make_async_copy(hay_at(b), hay_at(b), recv_hay.at[b]).wait()
        pass_on(lambda target: remote(hay_at(b), hay_at(b), send_hay.at[1], recv_hay.at[b], target).start())

        def per_chunk(c):
            ref = pbuf.at[b, :, rows_at(c)]
            pltpu.make_async_copy(ref, ref, recv_sem.at[b, c]).wait()
            pass_on(lambda target: remote(ref, ref, send_sem.at[1], recv_sem.at[b, c], target).start())

        each(CHUNKS, per_chunk)

    def res_copy(t, b, core):
        return remote(stage.at[t], res.at[stop], send_res, recv_res, b * 2 + core)

    partners = [0] * 64
    codes = [0] * (32 * ACTIONS)
    passed = [0] * 16
    results = [0] * 16
    for (blk, core), steps in UNITS.items():
        d = blk * 2 + core
        results[d] = 4 * len(steps) - (blk <= STOPS and core == 0)
        for t, (units, actions) in enumerate(steps):
            for u, i in enumerate(units):
                partners[d * 4 + t * 2 + u] = i + 1
            for n, (b, targets) in enumerate(actions):
                code = 0
                for target in reversed(targets):
                    code = code * 17 + target[0] * 2 + target[1] + 1
                codes[(d * 2 + t) * ACTIONS + n] = 1 + b + 8 * code
                passed[d] += len(targets)

    def prepare(i):
        mix_i = make_mix(hbuf[i, :count], spread[...], count)
        amp_i = dot_nn(mix_i, pbuf[i, 0]).astype(jnp.bfloat16)
        perm = dot_nn(jnp.concatenate([amp_i, pbuf[i, 1]], axis=0), sel[...])
        cond_t = perm[2 * edge :].T.astype(jnp.bfloat16)
        turned = jnp.concatenate([perm[edge : 2 * edge], -perm[:edge]], axis=0)
        both = jnp.concatenate([perm[: 2 * edge], turned], axis=1).astype(jnp.bfloat16)
        val_b = pbuf[(i + stop) % blocks, 0]
        swapped = jnp.concatenate([-val_b[edge:], val_b[:edge]], axis=0)
        v_lanes = jnp.concatenate(
            [
                jnp.concatenate([val_b[:edge], swapped[:edge]], axis=0),
                jnp.concatenate([val_b[edge:], swapped[edge:]], axis=0),
            ],
            axis=1,
        )
        return cond_t, both, v_lanes

    def fold_tile(cond_t, both, v_lanes, w):
        h = (dot_nn(cond_t, both) * jnp.concatenate([w, w], axis=1)).astype(jnp.bfloat16)
        return dot_nt(h, v_lanes).astype(jnp.bfloat16)

    def finish(t, i, f_rows):
        b = (i + stop) % blocks
        part = fold_block(dot_nn(pbuf[b, 1], f_rows), count) * scale_d
        stage[t, :, : 2 * edge] = part

        @pl.when((b == me) & (p == 0))
        def _():
            res[stop, :, : 2 * edge] = part

        def send_result(core):
            @pl.when(jnp.logical_not((b == me) & (p == core)))
            def _():
                res_copy(t, b, core).start()

        each(2, send_result)

    def pair(t, partner):
        ready = [prepare(partner[u]) for u in range(2)]
        tile = 256
        for r in range(planes // tile):
            rows = slice(r * tile, (r + 1) * tile)
            w = wbuf[rows, :].astype(jnp.float32)
            for u, (cond_t, both, v_lanes) in enumerate(ready):
                fbuf[u, rows, :] = fold_tile(cond_t[rows], both, v_lanes, w)
        for u in range(2):
            finish(2 * t + u, partner[u], fbuf[u])

    fifteen = xbuf.at[pl.ds(0, 15)]

    @pl.when(worker)
    def _():
        sel[...] = jnp.where(
            mbuf[pl.ds(stop, 1), :] == iota((planes, planes), 0), 1.0, 0.0
        ).astype(jnp.bfloat16)

        @pl.when(holder)
        def _():
            loads[4].wait()

        def step(t):
            def act(n):
                @pl.when((dev == hub) & (t == 0) & (n == 1))
                def _():
                    pltpu.make_async_copy(fifteen, fifteen, recv_x).wait()
                    coul_row = jnp.concatenate([coul[k : k + 1, :] for k in range(planes // 128)], axis=1)
                    ybuf[...] = jnp.sum(xbuf[...], axis=0) * coul_row * (0.5 * scale_x)
                    others(lambda d: y_copy(d).start())

                @pl.when((me == LENT_TO) & (t == 0) & (n == 1))
                def _():
                    take_own()

                code = lut((dev * 2 + t) * ACTIONS + n, codes)
                packed = jnp.maximum(code - 1, 0)
                onward = packed // 8

                def pass_on(start):
                    def per_target(slot):
                        target = onward // lut(slot, [1, 17, 289]) % 17

                        @pl.when(target > 0)
                        def _():
                            start(jnp.maximum(target - 1, 0))

                    each(3, per_target)

                @pl.when(code > 0)
                def _():
                    arrive(packed % 8, pass_on)

            each(ACTIONS, act)

            partner = [lut(dev * 4 + 2 * t + u, partners) - 1 for u in range(2)]

            @pl.when((me == LENT_TO) & (t == 0))
            def _():
                take_other()

            @pl.when(partner[0] >= 0)
            def _():
                pair(t, [jnp.maximum(i, 0) for i in partner])

        each(2, step)

    @pl.when(dev != hub)
    def _():
        pltpu.make_async_copy(ybuf, ybuf, recv_y).wait()

    y_re, y_im = ybuf[0:1, :], ybuf[1:2, :]
    v_re = pbuf[me, 0, :edge].astype(jnp.float32)
    v_im = pbuf[me, 0, edge:].astype(jnp.float32)
    f_rows = jnp.concatenate([y_re * v_re + y_im * v_im, y_im * v_re - y_re * v_im], axis=0)
    total = fold_block(dot_nt(pbuf[me, 1], f_rows.astype(jnp.bfloat16)), count)

    awaited = jnp.where((p == 0) & holder, STOPS, STOPS + 1)
    drained(awaited, STOPS + 1, lambda n: res.at[pl.ds(0, n)], recv_res)
    for s in range(STOPS + 1):
        total = total + res[s, :, : 2 * edge]
    out_ref[...] = lay_out(total, count)[:count]

    own_count = lut(me, [len(OWN[m]) for m in range(8)])
    drained(own_count, 3, lambda n: pbuf.at[pl.ds(0, n), 0], send_sem.at[0])
    drained(jnp.where(p == 0, own_count, 0), 3, lambda n: hbuf.at[pl.ds(0, n), pl.ds(0, count)], send_hay.at[0])
    passed = lut(dev, passed)
    drained(passed, 4, lambda n: pbuf.at[pl.ds(0, n)], send_sem.at[1])
    drained(passed, 4, lambda n: hbuf.at[pl.ds(0, n), pl.ds(0, count)], send_hay.at[1])

    @pl.when(dev != hub)
    def _():
        x_copy.wait_send()

    @pl.when(dev == hub)
    def _():
        pltpu.make_async_copy(fifteen, fifteen, send_y).wait()

    drained(lut(dev, results), 8, lambda n: stage.at[pl.ds(0, n)], send_res)

    @pl.when((me == LENT) | (me == LENT_TO))
    def _():
        pltpu.make_async_copy(wbuf.at[pl.ds(0, half)], wbuf.at[pl.ds(0, half)], send_w).wait()


def scales(planes, count, total_k):
    return (
        -1.0 / (8.0 * math.sqrt(planes * count * (STOPS + 1))),
        1.0 / (8.0 * math.sqrt(planes * total_k)),
    )


def rows_of(wave):
    count, _, _, planes = wave.shape
    rows = wave.reshape(count, 2, NV, 2, planes).transpose(1, 3, 0, 2, 4)
    return rows.reshape(2, 2 * count * NV, planes)


def per_device(wavefunc, haydock, screened, coulomb, umklapp_map):
    count, _, _, planes = wavefunc.shape
    blocks = lax.axis_size("blk")
    edge = count * NV
    scale_d, scale_x = scales(planes, count, count * blocks)
    dma = pltpu.SemaphoreType.DMA
    return pl.pallas_call(
        functools.partial(kernel, count, scale_d, scale_x),
        out_shape=jax.ShapeDtypeStruct((count, 128), jnp.float32),
        in_specs=[pl.BlockSpec(memory_space=pltpu.HBM)] * 5,
        out_specs=pl.BlockSpec(memory_space=pltpu.VMEM),
        scratch_shapes=[
            pltpu.VMEM((blocks, 2, 2 * edge, planes), jnp.bfloat16),
            pltpu.VMEM((blocks, 8, 128), jnp.float32),
            pltpu.VMEM((planes, planes), jnp.bfloat16),
            pltpu.VMEM((STOPS + 1, planes), jnp.int32),
            pltpu.VMEM((planes // 128, 128), jnp.float32),
            pltpu.VMEM((planes, planes), jnp.bfloat16),
            pltpu.VMEM((2, planes, 2 * edge), jnp.bfloat16),
            pltpu.VMEM((128, 256), jnp.bfloat16),
            pltpu.VMEM((8, 2 * NV, 128), jnp.float32),
            pltpu.VMEM((STOPS + 1, 2 * NV, 128), jnp.float32),
            pltpu.VMEM((2 * blocks, 2, planes), jnp.float32),
            pltpu.VMEM((2, planes), jnp.float32),
            dma((5,)),
            dma((blocks, CHUNKS)),
            dma((blocks,)),
            dma((2, WCHUNKS)),
            dma,
            dma((2,)),
            dma((2,)),
            dma,
            dma,
            dma,
            dma,
            dma,
            dma,
        ],
        compiler_params=pltpu.CompilerParams(
            collective_id=0, has_side_effects=True, vmem_limit_bytes=62 * 1024 * 1024
        ),
    )(rows_of(wavefunc), haydock, screened, umklapp_map, coulomb.reshape(-1, 128))


def make_pieces(wave, hay):
    count, bands, _, planes = wave.shape
    rows = wave.reshape(count, 2, NV, 2, planes).transpose(1, 3, 0, 2, 4)
    rows = rows.reshape(2, 2 * count * NV, planes)
    psi = hay.reshape(count, 2, NV, NC).transpose(1, 0, 3, 2)
    eye = jnp.eye(count, dtype=jnp.float32)
    wide = (psi[:, :, :, None, :] * eye[None, :, None, :, None]).reshape(2, count * NC, count * NV)
    top = jnp.concatenate([wide[0], -wide[1]], axis=1)
    low = jnp.concatenate([wide[1], wide[0]], axis=1)
    mix = jnp.concatenate([top, low], axis=0).astype(jnp.bfloat16)
    return rows, mix


def unpack_result(total, count):
    half = count * NC
    out_re = total[:NV, :half] - total[NV:, half : 2 * half]
    out_im = total[NV:, :half] + total[:NV, half : 2 * half]
    out = jnp.stack([out_re, out_im]).reshape(2, NV, count, NC)
    return out.transpose(2, 0, 1, 3).reshape(count, 2 * NV * NC)


def fold_rows(f_rows, cond, count):
    t = dot_nt(f_rows, cond)
    rows, lanes = t.shape
    keep = (lax.broadcasted_iota(jnp.int32, t.shape, 0) // NV) % count == (
        lax.broadcasted_iota(jnp.int32, t.shape, 1) // NC
    ) % count
    t = jnp.where(keep, t, 0.0).reshape(2, count, NV, lanes)
    return jnp.sum(t, axis=1).reshape(2 * NV, lanes)


def per_device_general(wavefunc, haydock, screened, coulomb, umklapp_map):
    count, _, _, planes = wavefunc.shape
    blocks = lax.axis_size("blk")
    edge = count * NV
    rows, mix = make_pieces(wavefunc, haydock)
    val, cond = rows[0], rows[1]
    amp = dot_nn(mix, val)
    wide = cond.astype(jnp.float32)
    c_re, c_im, a_re, a_im = wide[:edge], wide[edge:], amp[:edge], amp[edge:]
    x_re = jnp.sum(c_re * a_re + c_im * a_im, axis=0)
    x_im = jnp.sum(c_re * a_im - c_im * a_re, axis=0)
    xs = lax.psum(jnp.stack([x_re, x_im]), "blk")
    scale_d, scale_x = scales(planes, count, count * blocks)
    y = xs * coulomb * scale_x
    v_re, v_im = val[:edge].astype(jnp.float32), val[edge:].astype(jnp.float32)
    f = jnp.concatenate([y[0] * v_re + y[1] * v_im, y[1] * v_re - y[0] * v_im], axis=0)
    current = jnp.concatenate([amp.astype(jnp.bfloat16), cond], axis=0)
    for stop in range(STOPS + 1):
        if stop > 0:
            current = lax.ppermute(current, "blk", [(i, (i + 1) % blocks) for i in range(blocks)])
        held = lax.axis_index("blk") == stop
        weight = lax.psum(jnp.where(held, screened[0], jnp.zeros_like(screened[0])), "blk")
        pick = (umklapp_map[stop][:, None] == jnp.arange(planes)[None, :]).astype(jnp.bfloat16)
        perm = dot_nt(current, pick).astype(jnp.bfloat16)
        amp_p, cond_t = perm[: 2 * edge], perm[2 * edge :].T
        turned = jnp.concatenate([amp_p[edge:], -amp_p[:edge]], axis=0)
        h_re = (dot_nn(cond_t, amp_p) * weight.astype(jnp.float32)).astype(jnp.bfloat16)
        h_im = (dot_nn(cond_t, turned) * weight.astype(jnp.float32)).astype(jnp.bfloat16)
        g_re, g_im = dot_nt(val, h_re), dot_nt(val, h_im)
        f = f + scale_d * jnp.concatenate([g_re[:edge] + g_im[edge:], g_im[:edge] - g_re[edge:]], axis=0)
    return unpack_result(fold_rows(f.astype(jnp.bfloat16), cond, count), count)


def solution(mesh):
    placed = (
        P(("grp", "blk"), None, None, None),
        P(("grp", "blk"), None),
        P(("grp", "blk"), None, None),
        P("grp"),
        P(),
    )
    body = per_device if mesh.shape["blk"] == 8 and mesh.shape["pair"] == 2 else per_device_general
    return jax.shard_map(
        body, mesh=mesh, in_specs=placed, out_specs=P(("grp", "blk"), None), check_vma=False
    )
```

```python
import functools
import math

import jax
import jax.numpy as jnp
from jax import lax
from jax.experimental import pallas as pl
from jax.experimental.pallas import tpu as pltpu
from jax.sharding import PartitionSpec as P

NV = 8
NC = 8
STOPS = 2
MESH = pl.DeviceIdType.MESH
NT = (((1,), (1,)), ((), ()))

OWN = {
    0: ((1, 0), (2, 0)),
    1: ((0, 1),),
    2: ((0, 0),),
    3: ((1, 1), (2, 1)),
    4: ((2, 0),),
    5: ((3, 0),),
    6: ((2, 0),),
    7: ((3, 1),),
}
UNITS = {
    (0, 0): (((0, 2), ((2, ((1, 1),)),)), ((4, 6), ((4, ()), (6, ())))),
    (0, 1): (((1, 3), ((1, ((2, 1),)), (3, ()))), ((5, 7), ((5, ()), (7, ())))),
    (1, 0): (((0, 7), ((0, ()), (7, ((0, 1),)))),),
    (1, 1): (((1, 2), ((3, ((0, 1),)), (2, ()))),),
    (2, 0): (((6, 4), ((6, ((0, 0), (3, 1))), (4, ((0, 0), (3, 0))), (0, ()))), ((0, 2), ())),
    (2, 1): (((7, 1), ((3, ()), (1, ()), (7, ()))), ((3, 5), ((5, ()),))),
    (3, 0): (((3, 4), ((5, ((2, 1), (0, 1), (3, 1))), (4, ()))),),
    (3, 1): (((5, 6), ((7, ((1, 0), (2, 1))), (5, ()), (6, ()))),),
}
LENT = 1
LENT_TO = 3
WCHUNKS = 3
HUB = (0, 1)
ACTIONS = 3
CHUNKS = 3


def edges():
    to = {}
    for blk, targets in OWN.items():
        for target in targets:
            for core in range(2):
                to.setdefault(target, set()).add((blk, core))
    for worker, units in UNITS.items():
        for _, actions in units:
            for _, targets in actions:
                for target in targets:
                    to.setdefault(target, set()).add(worker)
    for core in range(2):
        to.setdefault((LENT_TO, core), set()).update({(LENT, core), (LENT_TO, 1 - core)})
    for blk in range(8):
        for core in range(2):
            if (blk, core) != HUB:
                to.setdefault(HUB, set()).add((blk, core))
    for blk in range(STOPS + 1):
        to.setdefault((blk, 1), set()).add((blk, 0))
    return to


def dot_nt(a, b):
    return lax.dot_general(a, b, NT, preferred_element_type=jnp.float32)


def dot_nn(a, b):
    return jnp.dot(a, b, preferred_element_type=jnp.float32)


def lut(index, values):
    out = jnp.int32(0)
    for n, value in enumerate(values):
        if value:
            out = jnp.where(index == n, jnp.int32(value), out)
    return out


def iota(shape, dim):
    return lax.broadcasted_iota(jnp.int32, shape, dim)


def spread_matrix(edge):
    half = edge
    row, col = iota((128, 256), 0), iota((128, 256), 1)
    lane = col % 128
    y = (lane >= half).astype(jnp.int32)
    part = jnp.where(col >= 128, 1 - y, y)
    return ((row // 64 == part) & ((row % 64) // NC == lane % NV)).astype(jnp.bfloat16)


def make_mix(hay, spread, count):
    edge = count * NV
    tall = jnp.concatenate(
        [jnp.broadcast_to(hay[k : k + 1, :], (NC, 128)) for _ in range(2) for k in range(count)], axis=0
    )
    shape = (2 * edge, 128)
    row, col = iota(shape, 0), iota(shape, 1)
    tall = jnp.where(row % NC == col % NC, tall, 0.0).astype(jnp.bfloat16)
    q = dot_nn(tall, spread)
    top = row < edge
    k_row = jnp.where(top, row, row - edge) // NC
    k_col = jnp.where(col < edge, col, col - edge) // NV
    mix = jnp.where(top, jnp.where(col < edge, q[:, :128], -q[:, :128]), q[:, 128:])
    keep = (k_row == k_col) & (col < 2 * edge)
    return jnp.where(keep, mix, 0.0).astype(jnp.bfloat16)[:, : 2 * edge]


def fold_block(t, count):
    edge = count * NV
    row, col = iota(t.shape, 0), iota(t.shape, 1)
    k_row = jnp.where(row < edge, row, row - edge) // NC
    k_col = jnp.where(col < edge, col, col - edge) // NV
    t = jnp.where(k_row == k_col, t, 0.0)
    halves = []
    for x in range(2):
        acc = t[x * edge : x * edge + NC]
        for k in range(1, count):
            acc = acc + t[x * edge + k * NC : x * edge + (k + 1) * NC]
        halves.append(acc)
    return jnp.concatenate(halves, axis=0)


def lay_out(total, count):
    edge = count * NV
    z0 = jnp.concatenate([total[:NC]] * 16, axis=0)
    z1 = jnp.concatenate([total[NC:]] * 16, axis=0)
    shape = z0.shape
    row, col = iota(shape, 0), iota(shape, 1)
    y0 = col < edge
    z = jnp.where(row < 64, jnp.where(y0, z0, -z1), jnp.where(y0, z1, z0))
    z = jnp.where((row % 64) // NC == col % NV, z, 0.0)
    high = z.astype(jnp.bfloat16)
    low = (z - high.astype(jnp.float32)).astype(jnp.bfloat16)
    krow, kcol = iota((8, shape[1]), 0), iota((8, shape[1]), 1)
    pick = (jnp.where(kcol < edge, kcol, kcol - edge) // NV == krow).astype(jnp.bfloat16)
    return dot_nt(pick, high) + dot_nt(pick, low)


def kernel(
    count, scale_d, scale_x,
    piece_ref, hay_ref, weight_ref, map_ref, coul_ref, out_ref,
    pbuf, hbuf, wbuf, mbuf, coul, sel, fbuf, spread, stage, res, xbuf, ybuf,
    load_sem, recv_sem, recv_hay, recv_w, send_w, send_sem, send_hay, send_res, recv_res, send_x, recv_x, send_y, recv_y,
):
    grp = lax.axis_index("grp")
    me = lax.axis_index("blk")
    p = lax.axis_index("pair")
    blocks = lax.axis_size("blk")
    dev = me * 2 + p
    planes = weight_ref.shape[1]
    edge = count * NV
    hub = HUB[0] * 2 + HUB[1]
    holder = me < STOPS + 1
    worker = holder | (me == LENT_TO)
    stop = jnp.where(me == LENT_TO, LENT, me)
    chunk = 2 * edge // CHUNKS

    def each(n, body):
        def wrapped(i, carry):
            body(i)
            return carry

        lax.fori_loop(0, n, wrapped, 0)

    barrier = pltpu.get_barrier_semaphore()
    to = edges()
    expect = [0] * 16
    masks = [0] * 16
    for (blk, core), senders in to.items():
        for sender in senders:
            expect[sender[0] * 2 + sender[1]] += 1
            masks[sender[0] * 2 + sender[1]] |= 1 << (blk * 2 + core)

    power = lut(dev, [1 << d for d in range(8)])

    def greet(other):
        @pl.when(lut(other, masks) // jnp.maximum(power, 1) % 2 == 1)
        def _():
            pl.semaphore_signal(barrier, inc=1, device_id=(grp, other // 2, other % 2), device_id_type=MESH)

    @pl.when(worker)
    def _():
        each(16, greet)

    loads = [
        pltpu.make_async_copy(src, dst, load_sem.at[n])
        for n, (src, dst) in enumerate(
            (
                (hay_ref, hbuf.at[me, pl.ds(0, count)]),
                (piece_ref, pbuf.at[me]),
                (map_ref, mbuf),
                (coul_ref, coul),
                (weight_ref.at[0], wbuf),
            )
        )
    ]
    for load in loads[:4]:
        load.start()

    @pl.when(holder)
    def _():
        loads[4].start()

    pl.semaphore_wait(barrier, lut(dev, expect))

    def rows_at(c):
        return pl.ds(pl.multiple_of(c * chunk, chunk), chunk)

    def hay_at(b):
        return hbuf.at[b, pl.ds(0, count)]

    def remote(src, dst, send, recv, target):
        return pltpu.make_async_remote_copy(
            src_ref=src, dst_ref=dst, send_sem=send, recv_sem=recv,
            device_id=(grp, target // 2, target % 2), device_id_type=MESH,
        )

    def drained(n, most, ref_of, sem):
        for m in range(1, most + 1):
            @pl.when(n == m)
            def _():
                pltpu.make_async_copy(ref_of(m), ref_of(m), sem).wait()

    own_targets = [0] * 24
    for m, targets in OWN.items():
        for slot, (blk, core) in enumerate(targets):
            own_targets[m * 3 + slot] = blk * 2 + core + 1

    def own_slot(slot):
        code = lut(me * 3 + slot, own_targets)
        target = jnp.maximum(code - 1, 0)

        @pl.when(code > 0)
        def _():
            @pl.when(p == 0)
            def _():
                remote(hay_ref, hay_at(me), send_hay.at[0], recv_hay.at[me], target).start()

            each(CHUNKS, lambda c: remote(
                piece_ref.at[p, rows_at(c)], pbuf.at[me, p, rows_at(c)],
                send_sem.at[0], recv_sem.at[me, c], target,
            ).start())

    half = planes // 2
    share = half // WCHUNKS

    def lent_rows(core, c):
        return pl.ds(pl.multiple_of(core * half + c * share, share), share)

    @pl.when(me == LENT)
    def _():
        each(WCHUNKS, lambda c: remote(
            weight_ref.at[0, lent_rows(p, c)], wbuf.at[lent_rows(p, c)],
            send_w, recv_w.at[p, c], LENT_TO * 2 + p,
        ).start())

    each(3, own_slot)

    def take_own():
        def per_chunk(c):
            ref = wbuf.at[lent_rows(p, c)]
            pltpu.make_async_copy(ref, ref, recv_w.at[p, c]).wait()
            remote(ref, ref, send_w, recv_w.at[p, c], LENT_TO * 2 + 1 - p).start()

        each(WCHUNKS, per_chunk)

    def take_other():
        def per_chunk(c):
            ref = wbuf.at[lent_rows(1 - p, c)]
            pltpu.make_async_copy(ref, ref, recv_w.at[1 - p, c]).wait()

        each(WCHUNKS, per_chunk)

    spread[...] = spread_matrix(edge)
    for load in loads[:4]:
        load.wait()
    mix = make_mix(hbuf[me, :count], spread[...], count)
    amp = dot_nn(mix, pbuf[me, 0])
    cond_own = pbuf[me, 1].astype(jnp.float32)
    c_re, c_im = cond_own[:edge], cond_own[edge:]
    a_re, a_im = amp[:edge], amp[edge:]
    xbuf[dev, 0:1, :] = jnp.sum(c_re * a_re + c_im * a_im, axis=0, keepdims=True)
    xbuf[dev, 1:2, :] = jnp.sum(c_re * a_im - c_im * a_re, axis=0, keepdims=True)
    x_copy = remote(xbuf.at[dev], xbuf.at[dev], send_x, recv_x, jnp.int32(hub))

    def others(body):
        def guarded(d):
            @pl.when(d != hub)
            def _():
                body(d)

        each(16, guarded)

    def y_copy(other):
        return remote(ybuf, ybuf, send_y, recv_y, other)

    @pl.when(dev != hub)
    def _():
        x_copy.start()

    def arrive(b, pass_on):
        pltpu.make_async_copy(hay_at(b), hay_at(b), recv_hay.at[b]).wait()
        pass_on(lambda target: remote(hay_at(b), hay_at(b), send_hay.at[1], recv_hay.at[b], target).start())

        def per_chunk(c):
            ref = pbuf.at[b, :, rows_at(c)]
            pltpu.make_async_copy(ref, ref, recv_sem.at[b, c]).wait()
            pass_on(lambda target: remote(ref, ref, send_sem.at[1], recv_sem.at[b, c], target).start())

        each(CHUNKS, per_chunk)

    def res_copy(t, b, core):
        return remote(stage.at[t], res.at[stop], send_res, recv_res, b * 2 + core)

    partners = [0] * 64
    codes = [0] * (32 * ACTIONS)
    passed = [0] * 16
    results = [0] * 16
    for (blk, core), steps in UNITS.items():
        d = blk * 2 + core
        results[d] = 4 * len(steps) - (blk <= STOPS and core == 0)
        for t, (units, actions) in enumerate(steps):
            for u, i in enumerate(units):
                partners[d * 4 + t * 2 + u] = i + 1
            for n, (b, targets) in enumerate(actions):
                code = 0
                for target in reversed(targets):
                    code = code * 17 + target[0] * 2 + target[1] + 1
                codes[(d * 2 + t) * ACTIONS + n] = 1 + b + 8 * code
                passed[d] += len(targets)

    def prepare(i):
        mix_i = make_mix(hbuf[i, :count], spread[...], count)
        amp_i = dot_nn(mix_i, pbuf[i, 0]).astype(jnp.bfloat16)
        perm = dot_nn(jnp.concatenate([amp_i, pbuf[i, 1]], axis=0), sel[...])
        cond_t = perm[2 * edge :].T.astype(jnp.bfloat16)
        turned = jnp.concatenate([perm[edge : 2 * edge], -perm[:edge]], axis=0)
        both = jnp.concatenate([perm[: 2 * edge], turned], axis=1).astype(jnp.bfloat16)
        val_b = pbuf[(i + stop) % blocks, 0]
        swapped = jnp.concatenate([-val_b[edge:], val_b[:edge]], axis=0)
        v_lanes = jnp.concatenate(
            [
                jnp.concatenate([val_b[:edge], swapped[:edge]], axis=0),
                jnp.concatenate([val_b[edge:], swapped[edge:]], axis=0),
            ],
            axis=1,
        )
        return cond_t, both, v_lanes

    def fold_tile(cond_t, both, v_lanes, w):
        h = (dot_nn(cond_t, both) * jnp.concatenate([w, w], axis=1)).astype(jnp.bfloat16)
        return dot_nt(h, v_lanes).astype(jnp.bfloat16)

    def finish(t, i, f_rows):
        b = (i + stop) % blocks
        part = fold_block(dot_nn(pbuf[b, 1], f_rows), count) * scale_d
        stage[t, :, : 2 * edge] = part

        @pl.when((b == me) & (p == 0))
        def _():
            res[stop, :, : 2 * edge] = part

        def send_result(core):
            @pl.when(jnp.logical_not((b == me) & (p == core)))
            def _():
                res_copy(t, b, core).start()

        each(2, send_result)

    def pair(t, partner):
        ready = [prepare(partner[u]) for u in range(2)]
        tile = 256
        for r in range(planes // tile):
            rows = slice(r * tile, (r + 1) * tile)
            w = wbuf[rows, :].astype(jnp.float32)
            for u, (cond_t, both, v_lanes) in enumerate(ready):
                fbuf[u, rows, :] = fold_tile(cond_t[rows], both, v_lanes, w)
        for u in range(2):
            finish(2 * t + u, partner[u], fbuf[u])

    fifteen = xbuf.at[pl.ds(0, 15)]

    @pl.when(worker)
    def _():
        sel[...] = jnp.where(
            mbuf[pl.ds(stop, 1), :] == iota((planes, planes), 0), 1.0, 0.0
        ).astype(jnp.bfloat16)

        @pl.when(holder)
        def _():
            loads[4].wait()

        def step(t):
            def act(n):
                @pl.when((dev == hub) & (t == 0) & (n == 1))
                def _():
                    pltpu.make_async_copy(fifteen, fifteen, recv_x).wait()
                    coul_row = jnp.concatenate([coul[k : k + 1, :] for k in range(planes // 128)], axis=1)
                    ybuf[...] = jnp.sum(xbuf[...], axis=0) * coul_row * (0.5 * scale_x)
                    others(lambda d: y_copy(d).start())

                @pl.when((me == LENT_TO) & (t == 0) & (n == 1))
                def _():
                    take_own()

                code = lut((dev * 2 + t) * ACTIONS + n, codes)
                packed = jnp.maximum(code - 1, 0)
                onward = packed // 8

                def pass_on(start):
                    def per_target(slot):
                        target = onward // lut(slot, [1, 17, 289]) % 17

                        @pl.when(target > 0)
                        def _():
                            start(jnp.maximum(target - 1, 0))

                    each(3, per_target)

                @pl.when(code > 0)
                def _():
                    arrive(packed % 8, pass_on)

            each(ACTIONS, act)

            partner = [lut(dev * 4 + 2 * t + u, partners) - 1 for u in range(2)]

            @pl.when((me == LENT_TO) & (t == 0))
            def _():
                take_other()

            @pl.when(partner[0] >= 0)
            def _():
                pair(t, [jnp.maximum(i, 0) for i in partner])

        each(2, step)

    @pl.when(dev != hub)
    def _():
        pltpu.make_async_copy(ybuf, ybuf, recv_y).wait()

    y_re, y_im = ybuf[0:1, :], ybuf[1:2, :]
    v_re = pbuf[me, 0, :edge].astype(jnp.float32)
    v_im = pbuf[me, 0, edge:].astype(jnp.float32)
    f_rows = jnp.concatenate([y_re * v_re + y_im * v_im, y_im * v_re - y_re * v_im], axis=0)
    total = fold_block(dot_nt(pbuf[me, 1], f_rows.astype(jnp.bfloat16)), count)

    awaited = jnp.where((p == 0) & holder, STOPS, STOPS + 1)
    drained(awaited, STOPS + 1, lambda n: res.at[pl.ds(0, n)], recv_res)
    for s in range(STOPS + 1):
        total = total + res[s, :, : 2 * edge]
    out_ref[...] = lay_out(total, count)[:count]

    own_count = lut(me, [len(OWN[m]) for m in range(8)])
    drained(own_count, 3, lambda n: pbuf.at[pl.ds(0, n), 0], send_sem.at[0])
    drained(jnp.where(p == 0, own_count, 0), 3, lambda n: hbuf.at[pl.ds(0, n), pl.ds(0, count)], send_hay.at[0])
    passed = lut(dev, passed)
    drained(passed, 4, lambda n: pbuf.at[pl.ds(0, n)], send_sem.at[1])
    drained(passed, 4, lambda n: hbuf.at[pl.ds(0, n), pl.ds(0, count)], send_hay.at[1])

    @pl.when(dev != hub)
    def _():
        x_copy.wait_send()

    @pl.when(dev == hub)
    def _():
        pltpu.make_async_copy(fifteen, fifteen, send_y).wait()

    drained(lut(dev, results), 8, lambda n: stage.at[pl.ds(0, n)], send_res)

    @pl.when((me == LENT) | (me == LENT_TO))
    def _():
        pltpu.make_async_copy(wbuf.at[pl.ds(0, half)], wbuf.at[pl.ds(0, half)], send_w).wait()


def scales(planes, count, total_k):
    return (
        -1.0 / (8.0 * math.sqrt(planes * count * (STOPS + 1))),
        1.0 / (8.0 * math.sqrt(planes * total_k)),
    )


def rows_of(wave):
    count, _, _, planes = wave.shape
    rows = wave.reshape(count, 2, NV, 2, planes).transpose(1, 3, 0, 2, 4)
    return rows.reshape(2, 2 * count * NV, planes)


def per_device(wavefunc, haydock, screened, coulomb, umklapp_map):
    count, _, _, planes = wavefunc.shape
    blocks = lax.axis_size("blk")
    edge = count * NV
    scale_d, scale_x = scales(planes, count, count * blocks)
    dma = pltpu.SemaphoreType.DMA
    return pl.pallas_call(
        functools.partial(kernel, count, scale_d, scale_x),
        out_shape=jax.ShapeDtypeStruct((count, 128), jnp.float32),
        in_specs=[pl.BlockSpec(memory_space=pltpu.HBM)] * 5,
        out_specs=pl.BlockSpec(memory_space=pltpu.VMEM),
        scratch_shapes=[
            pltpu.VMEM((blocks, 2, 2 * edge, planes), jnp.bfloat16),
            pltpu.VMEM((blocks, 8, 128), jnp.float32),
            pltpu.VMEM((planes, planes), jnp.bfloat16),
            pltpu.VMEM((STOPS + 1, planes), jnp.int32),
            pltpu.VMEM((planes // 128, 128), jnp.float32),
            pltpu.VMEM((planes, planes), jnp.bfloat16),
            pltpu.VMEM((2, planes, 2 * edge), jnp.bfloat16),
            pltpu.VMEM((128, 256), jnp.bfloat16),
            pltpu.VMEM((8, 2 * NV, 128), jnp.float32),
            pltpu.VMEM((STOPS + 1, 2 * NV, 128), jnp.float32),
            pltpu.VMEM((2 * blocks, 2, planes), jnp.float32),
            pltpu.VMEM((2, planes), jnp.float32),
            dma((5,)),
            dma((blocks, CHUNKS)),
            dma((blocks,)),
            dma((2, WCHUNKS)),
            dma,
            dma((2,)),
            dma((2,)),
            dma,
            dma,
            dma,
            dma,
            dma,
            dma,
        ],
        compiler_params=pltpu.CompilerParams(
            collective_id=0, has_side_effects=True, vmem_limit_bytes=62 * 1024 * 1024
        ),
    )(rows_of(wavefunc), haydock, screened, umklapp_map, coulomb.reshape(-1, 128))


def make_pieces(wave, hay):
    count, bands, _, planes = wave.shape
    rows = wave.reshape(count, 2, NV, 2, planes).transpose(1, 3, 0, 2, 4)
    rows = rows.reshape(2, 2 * count * NV, planes)
    psi = hay.reshape(count, 2, NV, NC).transpose(1, 0, 3, 2)
    eye = jnp.eye(count, dtype=jnp.float32)
    wide = (psi[:, :, :, None, :] * eye[None, :, None, :, None]).reshape(2, count * NC, count * NV)
    top = jnp.concatenate([wide[0], -wide[1]], axis=1)
    low = jnp.concatenate([wide[1], wide[0]], axis=1)
    mix = jnp.concatenate([top, low], axis=0).astype(jnp.bfloat16)
    return rows, mix


def unpack_result(total, count):
    half = count * NC
    out_re = total[:NV, :half] - total[NV:, half : 2 * half]
    out_im = total[NV:, :half] + total[:NV, half : 2 * half]
    out = jnp.stack([out_re, out_im]).reshape(2, NV, count, NC)
    return out.transpose(2, 0, 1, 3).reshape(count, 2 * NV * NC)


def fold_rows(f_rows, cond, count):
    t = dot_nt(f_rows, cond)
    rows, lanes = t.shape
    keep = (lax.broadcasted_iota(jnp.int32, t.shape, 0) // NV) % count == (
        lax.broadcasted_iota(jnp.int32, t.shape, 1) // NC
    ) % count
    t = jnp.where(keep, t, 0.0).reshape(2, count, NV, lanes)
    return jnp.sum(t, axis=1).reshape(2 * NV, lanes)


def per_device_general(wavefunc, haydock, screened, coulomb, umklapp_map):
    count, _, _, planes = wavefunc.shape
    blocks = lax.axis_size("blk")
    edge = count * NV
    rows, mix = make_pieces(wavefunc, haydock)
    val, cond = rows[0], rows[1]
    amp = dot_nn(mix, val)
    wide = cond.astype(jnp.float32)
    c_re, c_im, a_re, a_im = wide[:edge], wide[edge:], amp[:edge], amp[edge:]
    x_re = jnp.sum(c_re * a_re + c_im * a_im, axis=0)
    x_im = jnp.sum(c_re * a_im - c_im * a_re, axis=0)
    xs = lax.psum(jnp.stack([x_re, x_im]), "blk")
    scale_d, scale_x = scales(planes, count, count * blocks)
    y = xs * coulomb * scale_x
    v_re, v_im = val[:edge].astype(jnp.float32), val[edge:].astype(jnp.float32)
    f = jnp.concatenate([y[0] * v_re + y[1] * v_im, y[1] * v_re - y[0] * v_im], axis=0)
    current = jnp.concatenate([amp.astype(jnp.bfloat16), cond], axis=0)
    for stop in range(STOPS + 1):
        if stop > 0:
            current = lax.ppermute(current, "blk", [(i, (i + 1) % blocks) for i in range(blocks)])
        held = lax.axis_index("blk") == stop
        weight = lax.psum(jnp.where(held, screened[0], jnp.zeros_like(screened[0])), "blk")
        pick = (umklapp_map[stop][:, None] == jnp.arange(planes)[None, :]).astype(jnp.bfloat16)
        perm = dot_nt(current, pick).astype(jnp.bfloat16)
        amp_p, cond_t = perm[: 2 * edge], perm[2 * edge :].T
        turned = jnp.concatenate([amp_p[edge:], -amp_p[:edge]], axis=0)
        h_re = (dot_nn(cond_t, amp_p) * weight.astype(jnp.float32)).astype(jnp.bfloat16)
        h_im = (dot_nn(cond_t, turned) * weight.astype(jnp.float32)).astype(jnp.bfloat16)
        g_re, g_im = dot_nt(val, h_re), dot_nt(val, h_im)
        f = f + scale_d * jnp.concatenate([g_re[:edge] + g_im[edge:], g_im[:edge] - g_re[edge:]], axis=0)
    return unpack_result(fold_rows(f.astype(jnp.bfloat16), cond, count), count)


def solution(mesh):
    placed = (
        P(("grp", "blk"), None, None, None),
        P(("grp", "blk"), None),
        P(("grp", "blk"), None, None),
        P("grp"),
        P(),
    )
    body = per_device if mesh.shape["blk"] == 8 and mesh.shape["pair"] == 2 else per_device_general
    return jax.shard_map(
        body, mesh=mesh, in_specs=placed, out_specs=P(("grp", "blk"), None), check_vma=False
    )
```

```python
import functools
import math

import jax
import jax.numpy as jnp
from jax import lax
from jax.experimental import pallas as pl
from jax.experimental.pallas import tpu as pltpu
from jax.sharding import PartitionSpec as P

NV = 8
NC = 8
STOPS = 2
MESH = pl.DeviceIdType.MESH
NT = (((1,), (1,)), ((), ()))

OWN = {
    0: ((1, 0), (2, 0)),
    1: ((0, 1),),
    2: ((0, 0),),
    3: ((1, 1), (2, 1)),
    4: ((2, 0),),
    5: ((3, 0),),
    6: ((2, 0),),
    7: ((3, 1),),
}
UNITS = {
    (0, 0): (((0, 2), ((2, ((1, 1),)),)), ((6,), ((6, ()),)), ((4,), ((4, ()),))),
    (0, 1): (((1, 3), ((1, ((2, 1),)), (3, ()))), ((5,), ((5, ()),)), ((7,), ((7, ()),))),
    (1, 0): (((0, 7), ((0, ()), (7, ((0, 1),)))),),
    (1, 1): (((1, 2), ((3, ((0, 1),)), (2, ()))),),
    (2, 0): (((6, 4), ((6, ((0, 0), (3, 1))), (4, ((0, 0), (3, 0))), (0, ()))), ((0, 2), ())),
    (2, 1): (((7, 1), ((3, ()), (1, ()), (7, ()))), ((3, 5), ((5, ()),))),
    (3, 0): (((3, 4), ((5, ((2, 1), (0, 1), (3, 1))), (4, ()))),),
    (3, 1): (((5, 6), ((7, ((1, 0), (2, 1))), (5, ()), (6, ()))),),
}
LENT = 1
LENT_TO = 3
WCHUNKS = 3
HUB = (1, 0)
ACTIONS = 3
CHUNKS = 3


def edges():
    to = {}
    for blk, targets in OWN.items():
        for target in targets:
            for core in range(2):
                to.setdefault(target, set()).add((blk, core))
    for worker, units in UNITS.items():
        for _, actions in units:
            for _, targets in actions:
                for target in targets:
                    to.setdefault(target, set()).add(worker)
    for core in range(2):
        to.setdefault((LENT_TO, core), set()).update({(LENT, core), (LENT_TO, 1 - core)})
    for blk in range(8):
        for core in range(2):
            if (blk, core) != HUB:
                to.setdefault(HUB, set()).add((blk, core))
    for blk in range(STOPS + 1):
        to.setdefault((blk, 1), set()).add((blk, 0))
    return to


def dot_nt(a, b):
    return lax.dot_general(a, b, NT, preferred_element_type=jnp.float32)


def dot_nn(a, b):
    return jnp.dot(a, b, preferred_element_type=jnp.float32)


def lut(index, values):
    out = jnp.int32(0)
    for n, value in enumerate(values):
        if value:
            out = jnp.where(index == n, jnp.int32(value), out)
    return out


def iota(shape, dim):
    return lax.broadcasted_iota(jnp.int32, shape, dim)


def spread_matrix(edge):
    half = edge
    row, col = iota((128, 256), 0), iota((128, 256), 1)
    lane = col % 128
    y = (lane >= half).astype(jnp.int32)
    part = jnp.where(col >= 128, 1 - y, y)
    return ((row // 64 == part) & ((row % 64) // NC == lane % NV)).astype(jnp.bfloat16)


def make_mix(hay, spread, count):
    edge = count * NV
    tall = jnp.concatenate(
        [jnp.broadcast_to(hay[k : k + 1, :], (NC, 128)) for _ in range(2) for k in range(count)], axis=0
    )
    shape = (2 * edge, 128)
    row, col = iota(shape, 0), iota(shape, 1)
    tall = jnp.where(row % NC == col % NC, tall, 0.0).astype(jnp.bfloat16)
    q = dot_nn(tall, spread)
    top = row < edge
    k_row = jnp.where(top, row, row - edge) // NC
    k_col = jnp.where(col < edge, col, col - edge) // NV
    mix = jnp.where(top, jnp.where(col < edge, q[:, :128], -q[:, :128]), q[:, 128:])
    keep = (k_row == k_col) & (col < 2 * edge)
    return jnp.where(keep, mix, 0.0).astype(jnp.bfloat16)[:, : 2 * edge]


def fold_block(t, count):
    edge = count * NV
    row, col = iota(t.shape, 0), iota(t.shape, 1)
    k_row = jnp.where(row < edge, row, row - edge) // NC
    k_col = jnp.where(col < edge, col, col - edge) // NV
    t = jnp.where(k_row == k_col, t, 0.0)
    halves = []
    for x in range(2):
        acc = t[x * edge : x * edge + NC]
        for k in range(1, count):
            acc = acc + t[x * edge + k * NC : x * edge + (k + 1) * NC]
        halves.append(acc)
    return jnp.concatenate(halves, axis=0)


def lay_out(total, count):
    edge = count * NV
    z0 = jnp.concatenate([total[:NC]] * 16, axis=0)
    z1 = jnp.concatenate([total[NC:]] * 16, axis=0)
    shape = z0.shape
    row, col = iota(shape, 0), iota(shape, 1)
    y0 = col < edge
    z = jnp.where(row < 64, jnp.where(y0, z0, -z1), jnp.where(y0, z1, z0))
    z = jnp.where((row % 64) // NC == col % NV, z, 0.0)
    high = z.astype(jnp.bfloat16)
    low = (z - high.astype(jnp.float32)).astype(jnp.bfloat16)
    krow, kcol = iota((8, shape[1]), 0), iota((8, shape[1]), 1)
    pick = (jnp.where(kcol < edge, kcol, kcol - edge) // NV == krow).astype(jnp.bfloat16)
    return dot_nt(pick, high) + dot_nt(pick, low)


def kernel(
    count, scale_d, scale_x,
    piece_ref, hay_ref, weight_ref, map_ref, coul_ref, out_ref,
    pbuf, hbuf, wbuf, mbuf, coul, sel, fbuf, spread, stage, res, xbuf, ybuf,
    load_sem, recv_sem, recv_hay, recv_w, send_w, send_sem, send_hay, send_res, recv_res, send_x, recv_x, send_y, recv_y,
):
    grp = lax.axis_index("grp")
    me = lax.axis_index("blk")
    p = lax.axis_index("pair")
    blocks = lax.axis_size("blk")
    dev = me * 2 + p
    planes = weight_ref.shape[1]
    edge = count * NV
    hub = HUB[0] * 2 + HUB[1]
    holder = me < STOPS + 1
    worker = holder | (me == LENT_TO)
    stop = jnp.where(me == LENT_TO, LENT, me)
    chunk = 2 * edge // CHUNKS

    def each(n, body):
        def wrapped(i, carry):
            body(i)
            return carry

        lax.fori_loop(0, n, wrapped, 0)

    barrier = pltpu.get_barrier_semaphore()
    to = edges()
    expect = [0] * 16
    masks = [0] * 16
    for (blk, core), senders in to.items():
        for sender in senders:
            expect[sender[0] * 2 + sender[1]] += 1
            masks[sender[0] * 2 + sender[1]] |= 1 << (blk * 2 + core)

    power = lut(dev, [1 << d for d in range(8)])

    def greet(other):
        @pl.when(lut(other, masks) // jnp.maximum(power, 1) % 2 == 1)
        def _():
            pl.semaphore_signal(barrier, inc=1, device_id=(grp, other // 2, other % 2), device_id_type=MESH)

    @pl.when(worker)
    def _():
        each(16, greet)

    loads = [
        pltpu.make_async_copy(src, dst, load_sem.at[n])
        for n, (src, dst) in enumerate(
            (
                (hay_ref, hbuf.at[me, pl.ds(0, count)]),
                (piece_ref, pbuf.at[me]),
                (map_ref, mbuf),
                (coul_ref, coul),
                (weight_ref.at[0], wbuf),
            )
        )
    ]
    for load in loads[:4]:
        load.start()

    @pl.when(holder)
    def _():
        loads[4].start()

    pl.semaphore_wait(barrier, lut(dev, expect))

    def rows_at(c):
        return pl.ds(pl.multiple_of(c * chunk, chunk), chunk)

    def hay_at(b):
        return hbuf.at[b, pl.ds(0, count)]

    def remote(src, dst, send, recv, target):
        return pltpu.make_async_remote_copy(
            src_ref=src, dst_ref=dst, send_sem=send, recv_sem=recv,
            device_id=(grp, target // 2, target % 2), device_id_type=MESH,
        )

    def drained(n, most, ref_of, sem):
        for m in range(1, most + 1):
            @pl.when(n == m)
            def _():
                pltpu.make_async_copy(ref_of(m), ref_of(m), sem).wait()

    own_targets = [0] * 24
    for m, targets in OWN.items():
        for slot, (blk, core) in enumerate(targets):
            own_targets[m * 3 + slot] = blk * 2 + core + 1

    def own_slot(slot):
        code = lut(me * 3 + slot, own_targets)
        target = jnp.maximum(code - 1, 0)

        @pl.when(code > 0)
        def _():
            @pl.when(p == 0)
            def _():
                remote(hay_ref, hay_at(me), send_hay.at[0], recv_hay.at[me], target).start()

            each(CHUNKS, lambda c: remote(
                piece_ref.at[p, rows_at(c)], pbuf.at[me, p, rows_at(c)],
                send_sem.at[0], recv_sem.at[me, c], target,
            ).start())

    half = planes // 2
    share = half // WCHUNKS

    def lent_rows(core, c):
        return pl.ds(pl.multiple_of(core * half + c * share, share), share)

    @pl.when(me == LENT)
    def _():
        each(WCHUNKS, lambda c: remote(
            weight_ref.at[0, lent_rows(p, c)], wbuf.at[lent_rows(p, c)],
            send_w, recv_w.at[p, c], LENT_TO * 2 + p,
        ).start())

    each(3, own_slot)

    def take_own():
        def per_chunk(c):
            ref = wbuf.at[lent_rows(p, c)]
            pltpu.make_async_copy(ref, ref, recv_w.at[p, c]).wait()
            remote(ref, ref, send_w, recv_w.at[p, c], LENT_TO * 2 + 1 - p).start()

        each(WCHUNKS, per_chunk)

    def take_other():
        def per_chunk(c):
            ref = wbuf.at[lent_rows(1 - p, c)]
            pltpu.make_async_copy(ref, ref, recv_w.at[1 - p, c]).wait()

        each(WCHUNKS, per_chunk)

    spread[...] = spread_matrix(edge)
    for load in loads[:4]:
        load.wait()
    mix = make_mix(hbuf[me, :count], spread[...], count)
    amp = dot_nn(mix, pbuf[me, 0])
    cond_own = pbuf[me, 1].astype(jnp.float32)
    c_re, c_im = cond_own[:edge], cond_own[edge:]
    a_re, a_im = amp[:edge], amp[edge:]
    xbuf[dev, 0:1, :] = jnp.sum(c_re * a_re + c_im * a_im, axis=0, keepdims=True)
    xbuf[dev, 1:2, :] = jnp.sum(c_re * a_im - c_im * a_re, axis=0, keepdims=True)
    x_copy = remote(xbuf.at[dev], xbuf.at[dev], send_x, recv_x, jnp.int32(hub))

    def others(body):
        def guarded(d):
            @pl.when(d != hub)
            def _():
                body(d)

        each(16, guarded)

    def y_copy(other):
        return remote(ybuf, ybuf, send_y, recv_y, other)

    @pl.when(dev != hub)
    def _():
        x_copy.start()

    def arrive(b, pass_on):
        pltpu.make_async_copy(hay_at(b), hay_at(b), recv_hay.at[b]).wait()
        pass_on(lambda target: remote(hay_at(b), hay_at(b), send_hay.at[1], recv_hay.at[b], target).start())

        def per_chunk(c):
            ref = pbuf.at[b, :, rows_at(c)]
            pltpu.make_async_copy(ref, ref, recv_sem.at[b, c]).wait()
            pass_on(lambda target: remote(ref, ref, send_sem.at[1], recv_sem.at[b, c], target).start())

        each(CHUNKS, per_chunk)

    def res_copy(t, b, core):
        return remote(stage.at[t], res.at[stop], send_res, recv_res, b * 2 + core)

    partners = [0] * 96
    codes = [0] * (48 * ACTIONS)
    passed = [0] * 16
    results = [0] * 16
    for (blk, core), steps in UNITS.items():
        d = blk * 2 + core
        results[d] = 2 * sum(len(units) for units, _ in steps) - (blk <= STOPS and core == 0)
        for t, (units, actions) in enumerate(steps):
            for u, i in enumerate(units):
                partners[d * 6 + t * 2 + u] = i + 1
            for n, (b, targets) in enumerate(actions):
                code = 0
                for target in reversed(targets):
                    code = code * 17 + target[0] * 2 + target[1] + 1
                codes[(d * 3 + t) * ACTIONS + n] = 1 + b + 8 * code
                passed[d] += len(targets)

    def prepare(i):
        mix_i = make_mix(hbuf[i, :count], spread[...], count)
        amp_i = dot_nn(mix_i, pbuf[i, 0]).astype(jnp.bfloat16)
        perm = dot_nn(jnp.concatenate([amp_i, pbuf[i, 1]], axis=0), sel[...])
        cond_t = perm[2 * edge :].T.astype(jnp.bfloat16)
        turned = jnp.concatenate([perm[edge : 2 * edge], -perm[:edge]], axis=0)
        both = jnp.concatenate([perm[: 2 * edge], turned], axis=1).astype(jnp.bfloat16)
        val_b = pbuf[(i + stop) % blocks, 0]
        swapped = jnp.concatenate([-val_b[edge:], val_b[:edge]], axis=0)
        v_lanes = jnp.concatenate(
            [
                jnp.concatenate([val_b[:edge], swapped[:edge]], axis=0),
                jnp.concatenate([val_b[edge:], swapped[edge:]], axis=0),
            ],
            axis=1,
        )
        return cond_t, both, v_lanes

    def fold_tile(cond_t, both, v_lanes, w):
        h = (dot_nn(cond_t, both) * jnp.concatenate([w, w], axis=1)).astype(jnp.bfloat16)
        return dot_nt(h, v_lanes).astype(jnp.bfloat16)

    def finish(t, i, f_rows):
        b = (i + stop) % blocks
        part = fold_block(dot_nn(pbuf[b, 1], f_rows), count) * scale_d
        stage[t, :, : 2 * edge] = part

        @pl.when((b == me) & (p == 0))
        def _():
            res[stop, :, : 2 * edge] = part

        def send_result(core):
            @pl.when(jnp.logical_not((b == me) & (p == core)))
            def _():
                res_copy(t, b, core).start()

        each(2, send_result)

    def together(t, partner):
        ready = [prepare(i) for i in partner]
        tile = 256
        for r in range(planes // tile):
            rows = slice(r * tile, (r + 1) * tile)
            w = wbuf[rows, :].astype(jnp.float32)
            for u, (cond_t, both, v_lanes) in enumerate(ready):
                fbuf[u, rows, :] = fold_tile(cond_t[rows], both, v_lanes, w)
        for u, i in enumerate(partner):
            finish(2 * t + u, i, fbuf[u])

    fifteen = xbuf.at[pl.ds(0, 15)]

    @pl.when(worker)
    def _():
        sel[...] = jnp.where(
            mbuf[pl.ds(stop, 1), :] == iota((planes, planes), 0), 1.0, 0.0
        ).astype(jnp.bfloat16)

        @pl.when(holder)
        def _():
            loads[4].wait()

        def step(t):
            def act(n):
                @pl.when((dev == hub) & (t == 0) & (n == 1))
                def _():
                    pltpu.make_async_copy(fifteen, fifteen, recv_x).wait()
                    coul_row = jnp.concatenate([coul[k : k + 1, :] for k in range(planes // 128)], axis=1)
                    ybuf[...] = jnp.sum(xbuf[...], axis=0) * coul_row * (0.5 * scale_x)
                    others(lambda d: y_copy(d).start())

                @pl.when((me == LENT_TO) & (t == 0) & (n == 1))
                def _():
                    take_own()

                code = lut((dev * 3 + t) * ACTIONS + n, codes)
                packed = jnp.maximum(code - 1, 0)
                onward = packed // 8

                def pass_on(start):
                    def per_target(slot):
                        target = onward // lut(slot, [1, 17, 289]) % 17

                        @pl.when(target > 0)
                        def _():
                            start(jnp.maximum(target - 1, 0))

                    each(3, per_target)

                @pl.when(code > 0)
                def _():
                    arrive(packed % 8, pass_on)

            each(ACTIONS, act)

            partner = [lut(dev * 6 + 2 * t + u, partners) - 1 for u in range(2)]

            @pl.when((me == LENT_TO) & (t == 0))
            def _():
                take_other()

            for n in (1, 2):
                @pl.when((partner[0] >= 0) & ((partner[1] >= 0) == (n == 2)))
                def _():
                    together(t, [jnp.maximum(i, 0) for i in partner[:n]])

        each(3, step)

    @pl.when(dev != hub)
    def _():
        pltpu.make_async_copy(ybuf, ybuf, recv_y).wait()

    y_re, y_im = ybuf[0:1, :], ybuf[1:2, :]
    v_re = pbuf[me, 0, :edge].astype(jnp.float32)
    v_im = pbuf[me, 0, edge:].astype(jnp.float32)
    f_rows = jnp.concatenate([y_re * v_re + y_im * v_im, y_im * v_re - y_re * v_im], axis=0)
    total = fold_block(dot_nt(pbuf[me, 1], f_rows.astype(jnp.bfloat16)), count)

    awaited = jnp.where((p == 0) & holder, STOPS, STOPS + 1)
    drained(awaited, STOPS + 1, lambda n: res.at[pl.ds(0, n)], recv_res)
    for s in range(STOPS + 1):
        total = total + res[s, :, : 2 * edge]
    out_ref[...] = lay_out(total, count)[:count]

    own_count = lut(me, [len(OWN[m]) for m in range(8)])
    drained(own_count, 3, lambda n: pbuf.at[pl.ds(0, n), 0], send_sem.at[0])
    drained(jnp.where(p == 0, own_count, 0), 3, lambda n: hbuf.at[pl.ds(0, n), pl.ds(0, count)], send_hay.at[0])
    passed = lut(dev, passed)
    drained(passed, 4, lambda n: pbuf.at[pl.ds(0, n)], send_sem.at[1])
    drained(passed, 4, lambda n: hbuf.at[pl.ds(0, n), pl.ds(0, count)], send_hay.at[1])

    @pl.when(dev != hub)
    def _():
        x_copy.wait_send()

    @pl.when(dev == hub)
    def _():
        pltpu.make_async_copy(fifteen, fifteen, send_y).wait()

    drained(lut(dev, results), 8, lambda n: stage.at[pl.ds(0, n)], send_res)

    @pl.when((me == LENT) | (me == LENT_TO))
    def _():
        pltpu.make_async_copy(wbuf.at[pl.ds(0, half)], wbuf.at[pl.ds(0, half)], send_w).wait()


def scales(planes, count, total_k):
    return (
        -1.0 / (8.0 * math.sqrt(planes * count * (STOPS + 1))),
        1.0 / (8.0 * math.sqrt(planes * total_k)),
    )


def rows_of(wave):
    count, _, _, planes = wave.shape
    rows = wave.reshape(count, 2, NV, 2, planes).transpose(1, 3, 0, 2, 4)
    return rows.reshape(2, 2 * count * NV, planes)


def per_device(wavefunc, haydock, screened, coulomb, umklapp_map):
    count, _, _, planes = wavefunc.shape
    blocks = lax.axis_size("blk")
    edge = count * NV
    scale_d, scale_x = scales(planes, count, count * blocks)
    dma = pltpu.SemaphoreType.DMA
    return pl.pallas_call(
        functools.partial(kernel, count, scale_d, scale_x),
        out_shape=jax.ShapeDtypeStruct((count, 128), jnp.float32),
        in_specs=[pl.BlockSpec(memory_space=pltpu.HBM)] * 5,
        out_specs=pl.BlockSpec(memory_space=pltpu.VMEM),
        scratch_shapes=[
            pltpu.VMEM((blocks, 2, 2 * edge, planes), jnp.bfloat16),
            pltpu.VMEM((blocks, 8, 128), jnp.float32),
            pltpu.VMEM((planes, planes), jnp.bfloat16),
            pltpu.VMEM((STOPS + 1, planes), jnp.int32),
            pltpu.VMEM((planes // 128, 128), jnp.float32),
            pltpu.VMEM((planes, planes), jnp.bfloat16),
            pltpu.VMEM((2, planes, 2 * edge), jnp.bfloat16),
            pltpu.VMEM((128, 256), jnp.bfloat16),
            pltpu.VMEM((8, 2 * NV, 128), jnp.float32),
            pltpu.VMEM((STOPS + 1, 2 * NV, 128), jnp.float32),
            pltpu.VMEM((2 * blocks, 2, planes), jnp.float32),
            pltpu.VMEM((2, planes), jnp.float32),
            dma((5,)),
            dma((blocks, CHUNKS)),
            dma((blocks,)),
            dma((2, WCHUNKS)),
            dma,
            dma((2,)),
            dma((2,)),
            dma,
            dma,
            dma,
            dma,
            dma,
            dma,
        ],
        compiler_params=pltpu.CompilerParams(
            collective_id=0, has_side_effects=True, vmem_limit_bytes=62 * 1024 * 1024
        ),
    )(rows_of(wavefunc), haydock, screened, umklapp_map, coulomb.reshape(-1, 128))


def make_pieces(wave, hay):
    count, bands, _, planes = wave.shape
    rows = wave.reshape(count, 2, NV, 2, planes).transpose(1, 3, 0, 2, 4)
    rows = rows.reshape(2, 2 * count * NV, planes)
    psi = hay.reshape(count, 2, NV, NC).transpose(1, 0, 3, 2)
    eye = jnp.eye(count, dtype=jnp.float32)
    wide = (psi[:, :, :, None, :] * eye[None, :, None, :, None]).reshape(2, count * NC, count * NV)
    top = jnp.concatenate([wide[0], -wide[1]], axis=1)
    low = jnp.concatenate([wide[1], wide[0]], axis=1)
    mix = jnp.concatenate([top, low], axis=0).astype(jnp.bfloat16)
    return rows, mix


def unpack_result(total, count):
    half = count * NC
    out_re = total[:NV, :half] - total[NV:, half : 2 * half]
    out_im = total[NV:, :half] + total[:NV, half : 2 * half]
    out = jnp.stack([out_re, out_im]).reshape(2, NV, count, NC)
    return out.transpose(2, 0, 1, 3).reshape(count, 2 * NV * NC)


def fold_rows(f_rows, cond, count):
    t = dot_nt(f_rows, cond)
    rows, lanes = t.shape
    keep = (lax.broadcasted_iota(jnp.int32, t.shape, 0) // NV) % count == (
        lax.broadcasted_iota(jnp.int32, t.shape, 1) // NC
    ) % count
    t = jnp.where(keep, t, 0.0).reshape(2, count, NV, lanes)
    return jnp.sum(t, axis=1).reshape(2 * NV, lanes)


def per_device_general(wavefunc, haydock, screened, coulomb, umklapp_map):
    count, _, _, planes = wavefunc.shape
    blocks = lax.axis_size("blk")
    edge = count * NV
    rows, mix = make_pieces(wavefunc, haydock)
    val, cond = rows[0], rows[1]
    amp = dot_nn(mix, val)
    wide = cond.astype(jnp.float32)
    c_re, c_im, a_re, a_im = wide[:edge], wide[edge:], amp[:edge], amp[edge:]
    x_re = jnp.sum(c_re * a_re + c_im * a_im, axis=0)
    x_im = jnp.sum(c_re * a_im - c_im * a_re, axis=0)
    xs = lax.psum(jnp.stack([x_re, x_im]), "blk")
    scale_d, scale_x = scales(planes, count, count * blocks)
    y = xs * coulomb * scale_x
    v_re, v_im = val[:edge].astype(jnp.float32), val[edge:].astype(jnp.float32)
    f = jnp.concatenate([y[0] * v_re + y[1] * v_im, y[1] * v_re - y[0] * v_im], axis=0)
    current = jnp.concatenate([amp.astype(jnp.bfloat16), cond], axis=0)
    for stop in range(STOPS + 1):
        if stop > 0:
            current = lax.ppermute(current, "blk", [(i, (i + 1) % blocks) for i in range(blocks)])
        held = lax.axis_index("blk") == stop
        weight = lax.psum(jnp.where(held, screened[0], jnp.zeros_like(screened[0])), "blk")
        pick = (umklapp_map[stop][:, None] == jnp.arange(planes)[None, :]).astype(jnp.bfloat16)
        perm = dot_nt(current, pick).astype(jnp.bfloat16)
        amp_p, cond_t = perm[: 2 * edge], perm[2 * edge :].T
        turned = jnp.concatenate([amp_p[edge:], -amp_p[:edge]], axis=0)
        h_re = (dot_nn(cond_t, amp_p) * weight.astype(jnp.float32)).astype(jnp.bfloat16)
        h_im = (dot_nn(cond_t, turned) * weight.astype(jnp.float32)).astype(jnp.bfloat16)
        g_re, g_im = dot_nt(val, h_re), dot_nt(val, h_im)
        f = f + scale_d * jnp.concatenate([g_re[:edge] + g_im[edge:], g_im[:edge] - g_re[edge:]], axis=0)
    return unpack_result(fold_rows(f.astype(jnp.bfloat16), cond, count), count)


def solution(mesh):
    placed = (
        P(("grp", "blk"), None, None, None),
        P(("grp", "blk"), None),
        P(("grp", "blk"), None, None),
        P("grp"),
        P(),
    )
    body = per_device if mesh.shape["blk"] == 8 and mesh.shape["pair"] == 2 else per_device_general
    return jax.shard_map(
        body, mesh=mesh, in_specs=placed, out_specs=P(("grp", "blk"), None), check_vma=False
    )
```
